32 devices in a mesh: dp: 16 (over z, y, x), mp: 2 (over core).
Axes of the slice: x: 2, y: 2, z: 4, core: 2. Of those that a mesh axis runs over, the one named last changes fastest.
Arguments:
- tokens: bfloat16 [32768, 768], P(('dp', 'mp')), may hold values from -6 to 6
- cotangent: bfloat16 [32768, 768], P(('dp', 'mp')), may hold values from -6 to 6
- w_query: bfloat16 [768, 768], P(None, 'mp'), may hold values from -0.21875 to 0.21875
- key_projection_weight: bfloat16 [768, 768], P(None, 'mp'), may hold values from -0.21875 to 0.21875
- value_projection_weight: bfloat16 [768, 768], P(None, 'mp'), may hold values from -0.21875 to 0.21875
- w_out: bfloat16 [768, 768], P('mp'), may hold values from -1.25 to 1.25
- w_up: bfloat16 [768, 3072], P(None, 'mp'), may hold values from -0.21875 to 0.21875
- w_down: bfloat16 [3072, 768], P('mp'), may hold values from -0.109375 to 0.109375
- gain_attn: float32 [768], replicated, may hold values from 0.5 to 1.5
- gain_ffn: float32 [768], replicated, may hold values from 0.5 to 1.5
- value_pool: bfloat16 [128, 32, 768], P('dp'), may hold values from -6 to 6
- slot_index: int32 [128, 20], P('dp'), may hold values from 0 to 31
- slot_count: int32 [128], P('dp'), may hold values from 5 to 20
- pad_mask: int32 [128, 256], P('dp'), may hold values from 0 to 1, as said below
Outputs:
- block_out: bfloat16 [32768, 768], P(('dp', 'mp'))
- grad_tokens: float32 [32768, 768], P(('dp', 'mp'))
- grad_w_query: float32 [768, 768], P(None, 'mp')
- grad_w_key: float32 [768, 768], P(None, 'mp')
- grad_w_value: float32 [768, 768], P(None, 'mp')
- grad_w_out: float32 [768, 768], P('mp')
- grad_w_up: float32 [768, 3072], P(None, 'mp')
- grad_w_down: float32 [3072, 768], P('mp')
- grad_gain_attn: float32 [768], replicated
- grad_gain_ffn: float32 [768], replicated
- grad_value_pool: float32 [128, 32, 768], P('dp')
The draws below stay inside these ranges and needn't reach their ends.
Inputs may be any that keep to these rules, and one draw needn't show every extreme that they name: `pad_mask`: each row is ones from its first position on and zeros after them, with at least 32 ones.
All inputs are finite; a program needn't handle non-finite values.
Results may differ from the reference program's by a relative error of at most 0.018.
Values may be sent and summed in bfloat16 or wider, within the bound.
No kernel may reach another device: no remote copies, remote signals or barrier semaphores. Data moves between devices by JAX's collectives and lax.ppermute only.
A program may use at most 192 MiB of HBM per device.

```python
import jax
import jax.numpy as jnp
from jax import lax

D = 768
HEADS = 12
HDIM = 64
FF = 3072
SLOTS = 20
POOL = 32
LEN = 256
SEQS = 128
TOKENS = 32768


def task_kinds(key):
    kinds = jax.random.randint(jax.random.fold_in(key, 101), (SEQS,), 0, 3)
    return kinds.at[0].set(0)


def draw_slot_count(key, part):
    kinds = task_kinds(key)
    limits = jnp.array([SLOTS, SLOTS // 2, SLOTS * 4 // 5], dtype=jnp.int32)
    ceiling = limits[kinds]
    dropped = jax.random.randint(jax.random.fold_in(key, 202), (SEQS,), 0, ceiling // 2 + 1)
    counts = ceiling - dropped
    counts = counts.at[0].set(SLOTS)
    counts = counts.at[1].set(SLOTS // 2 - SLOTS // 4)
    return counts.astype(jnp.int32)


def draw_pad_mask(key, part):
    kinds = task_kinds(key)
    limits = jnp.array([LEN // 4, LEN, LEN // 2], dtype=jnp.int32)
    ceiling = limits[kinds]
    dropped = jax.random.randint(jax.random.fold_in(key, 303), (SEQS,), 0, ceiling // 2 + 1)
    lengths = ceiling - dropped
    positions = jnp.arange(LEN, dtype=jnp.int32)
    return (positions[None, :] < lengths[:, None]).astype(jnp.int32)


def touch_ends(entries, stream_key, smallest, top_value):
    longest = entries.shape.index(max(entries.shape))
    spots = []
    for shift in (0, 1):
        where = [jax.random.randint(jax.random.fold_in(stream_key, axis), (), 0, length) for axis, length in enumerate(entries.shape)]
        where[longest] = (where[longest] + shift) % entries.shape[longest]
        spots.append(tuple(where))
    return entries.at[spots[0]].set(smallest).at[spots[1]].set(top_value)


def shard_levels(own_key, extent, cuts, least, largest):
    level, own = 1.0, jax.random.fold_in(own_key, 6)
    for axis_at, shards_of in cuts:
        draws = jnp.exp(jax.random.uniform(jax.random.fold_in(own, axis_at), (shards_of,), jnp.float32, least / len(cuts), largest / len(cuts)))
        level = level * jnp.repeat(draws, extent[axis_at] // shards_of).reshape([-1 if axis == axis_at else 1 for axis in range(len(extent))])
    return level


def noise(key, extent, spread, most, cuts=(), held_as=jnp.bfloat16):
    values = jax.random.normal(key, extent, jnp.float32) * spread
    if len(cuts) > 0:
        values = shard_levels(key, extent, cuts, -0.22, 0.18) * values
    return jnp.clip(values, min=-most, max=most).astype(held_as)


def setup_inputs(seed: int = 0) -> dict:
    key_list = jax.random.split(jax.random.key(seed), 15)
    return {
        "tokens": noise(key_list[0], (TOKENS, D), 1.0, 6.0, ((0, 32),)),
        "cotangent": noise(key_list[1], (TOKENS, D), 1.0, 6.0, ((0, 32),)),
        "w_query": noise(key_list[2], (D, HEADS * HDIM), D ** -0.5, 0.21875, ((1, 2),)),
        "key_projection_weight": noise(key_list[3], (D, HEADS * HDIM), D ** -0.5, 0.21875, ((1, 2),)),
        "value_projection_weight": noise(key_list[4], (D, HEADS * HDIM), D ** -0.5, 0.21875, ((1, 2),)),
        "w_out": noise(key_list[5], (HEADS * HDIM, D), (HEADS * HDIM // 32) ** -0.5, 1.25, ((0, 2),)),
        "w_up": noise(key_list[6], (D, FF), D ** -0.5, 0.21875, ((1, 2),)),
        "w_down": noise(key_list[7], (FF, D), FF ** -0.5, 0.109375, ((0, 2),)),
        "gain_attn": jnp.clip(1.0 + 0.1 * jax.random.normal(key_list[8], (D,), jnp.float32), 0.5, 1.5),
        "gain_ffn": jnp.clip(1.0 + 0.1 * jax.random.normal(key_list[9], (D,), jnp.float32), 0.5, 1.5),
        "value_pool": noise(key_list[10], (SEQS, POOL, D), 1.0, 6.0, ((0, 16),)),
        "slot_index": touch_ends(jax.random.randint(key_list[11], (SEQS, SLOTS), 0, POOL), jax.random.fold_in(key_list[11], 1), 0, POOL - 1).astype(jnp.int32),
        "slot_count": draw_slot_count(jax.random.fold_in(key_list[14], 71), 0),
        "pad_mask": draw_pad_mask(jax.random.fold_in(key_list[14], 71), 0),
    }


@jax.custom_vjp
def low(v):
    return lax.optimization_barrier(v.astype(jnp.bfloat16)).astype(jnp.float32)

@jax.custom_vjp
def low_back(v):
    return v

def low_keep(v):
    return (low(v), None)

def low_pass(kept, grad):
    return (grad,)

def back_keep(v):
    return (v, None)

def back_low(kept, grad):
    return (low(grad),)
low.defvjp(low_keep, low_pass)
low_back.defvjp(back_keep, back_low)

def matmul(left, right):
    return jnp.dot(left, right, precision=lax.Precision.HIGHEST)

def rms_norm(rows, gain):
    factor = lax.rsqrt(lax.optimization_barrier(jnp.mean(rows * rows, axis=-1, keepdims=True)) + 1e-06)
    return rows * factor * gain

def attend_group(group):
    queries, projected_key_rows, projected_value_rows, key_valid = group
    scores = jnp.einsum('bqhd,bkhd->bhqk', queries, projected_key_rows, precision=lax.Precision.HIGHEST) * HDIM ** (-0.5)
    scores = low_back(scores)
    scores = jnp.where(key_valid[:, None, None, :], scores, -1000000000.0)
    row_peak = lax.optimization_barrier(jnp.max(scores, axis=-1, keepdims=True))
    raised = jnp.exp(scores - row_peak)
    attn_probs = raised / lax.optimization_barrier(jnp.sum(raised, axis=-1, keepdims=True))
    attn_probs = low(attn_probs)
    return jnp.einsum('bhqk,bkhd->bqhd', attn_probs, projected_value_rows, precision=lax.Precision.HIGHEST)

def reference(tokens, cotangent, w_query, key_projection_weight, value_projection_weight, w_out, w_up, w_down, gain_attn, gain_ffn, value_pool, slot_index, slot_count, pad_mask):
    pool_ids = jnp.arange(POOL, dtype=jnp.int32)
    onehot = (slot_index[:, :, None] == pool_ids[None, None, :]).astype(jnp.float32)
    slot_ids = jnp.arange(SLOTS, dtype=jnp.int32)
    key_valid = jnp.concatenate([slot_ids[None, :] < slot_count[:, None], pad_mask > 0], axis=1)
    group_count = SEQS // 16

    def forward(tokens_f, query_w, key_weight_matrix, value_weight_matrix, out_w, up_w, down_w, attn_gain, ffn_gain, pool_f):
        normed = low(rms_norm(tokens_f, attn_gain))
        queries = low(low_back(matmul(normed, query_w)))
        selected = jnp.einsum('bsp,bpd->bsd', onehot, pool_f, precision=lax.Precision.HIGHEST)
        key_source_input = jnp.concatenate([selected, normed.reshape(SEQS, LEN, D)], axis=1)
        projected_key_rows = low(low_back(jnp.einsum('guf,fi->gui', key_source_input, key_weight_matrix, precision=lax.Precision.HIGHEST)))
        projected_value_rows = low(low_back(jnp.einsum('guf,fi->gui', key_source_input, value_weight_matrix, precision=lax.Precision.HIGHEST)))
        mixed_heads = lax.map(jax.checkpoint(attend_group), (queries.reshape(group_count, 16, LEN, HEADS, HDIM), projected_key_rows.reshape(group_count, 16, SLOTS + LEN, HEADS, HDIM), projected_value_rows.reshape(group_count, 16, SLOTS + LEN, HEADS, HDIM), key_valid.reshape(group_count, 16, SLOTS + LEN)))
        mixed_heads = low(low_back(mixed_heads.reshape(SEQS * LEN, HEADS * HDIM)))
        middle = tokens_f + low_back(matmul(mixed_heads, out_w))
        normed_ffn = low(rms_norm(middle, ffn_gain))
        ffn_inner = low_back(matmul(normed_ffn, up_w))
        active = low(jax.nn.gelu(ffn_inner, approximate=True))
        return middle + low_back(matmul(active, down_w))
    primals = (tokens.astype(jnp.float32), w_query.astype(jnp.float32), key_projection_weight.astype(jnp.float32), value_projection_weight.astype(jnp.float32), w_out.astype(jnp.float32), w_up.astype(jnp.float32), w_down.astype(jnp.float32), gain_attn.astype(jnp.float32), gain_ffn.astype(jnp.float32), value_pool.astype(jnp.float32))
    block_f, pullback = jax.vjp(forward, *primals)
    grads = pullback(cotangent.astype(jnp.float32))
    return (block_f.astype(jnp.bfloat16), grads[0], grads[1], grads[2], grads[3], grads[4], grads[5], grads[6], grads[7], grads[8], grads[9])
```

```python
import functools

import jax
import jax.numpy as jnp
from jax import lax
from jax.experimental import pallas as pl
from jax.experimental.pallas import tpu as pltpu
from jax.sharding import PartitionSpec as P

HDIM = 64
EPS = 1e-06
SLOT_ROWS = 32
BF = jnp.bfloat16
F32 = jnp.float32
VMEM_LIMIT = 58 << 20

NN = (((1,), (0,)), ((), ()))
NT = (((1,), (1,)), ((), ()))
TN = (((0,), (0,)), ((), ()))


def mm(left, right, dims=NN):
    return lax.dot_general(left, right, dims, preferred_element_type=F32)


def params():
    return pltpu.CompilerParams(vmem_limit_bytes=VMEM_LIMIT)


def whole(shape):
    zeros = (0,) * len(shape)
    return pl.BlockSpec(shape, lambda *_: zeros)


def rows_of(rows, width):
    return pl.BlockSpec((rows, width), lambda s: (s, 0))


def seq_of(*shape):
    tail = (0,) * len(shape)
    return pl.BlockSpec((1, *shape), lambda s: (s, *tail))


def head_masks():
    lanes = lax.broadcasted_iota(jnp.int32, (1, 2 * HDIM), 1)
    return lanes < HDIM, lanes >= HDIM


def attend(q, k, v, bias, probs_ref):
    masks = head_masks()
    pieces = []
    for pair in range(q.shape[1] // (2 * HDIM)):
        cols = slice(pair * 2 * HDIM, (pair + 1) * 2 * HDIM)
        qp, kp, vp = q[:, cols], k[:, cols], v[:, cols]
        mixed = None
        for half, mask in enumerate(masks):
            scores = mm(kp, jnp.where(mask, qp, 0), NT) + bias
            peak = jnp.max(scores, axis=0, keepdims=True)
            raised = jnp.exp(scores - peak)
            total = jnp.sum(raised, axis=0, keepdims=True)
            probs = (raised * (1.0 / total)).astype(BF)
            probs_ref[0, 2 * pair + half] = probs
            part = mm(probs, jnp.where(mask, vp, 0), TN)
            mixed = part if mixed is None else mixed + part
        pieces.append(mixed.astype(BF))
    return jnp.concatenate(pieces, axis=1)


def project(xn, sel, wq, wk, wv, scale):
    rows = jnp.concatenate([xn, sel], axis=0)
    q = (mm(xn, wq) * scale).astype(BF)
    k = mm(rows, wk).astype(BF)
    v = mm(rows, wv).astype(BF)
    return q, k, v


def attn_first_kernel(
    scale, x_ref, gain_ref, pool_ref, idx_ref, bias_ref, wq_ref, wk_ref, wv_ref, wo_ref,
    xn_ref, sel_ref, q_ref, k_ref, v_ref, probs_ref, mixed_ref, part_ref,
):
    x = x_ref[...].astype(F32)
    factor = lax.rsqrt(jnp.mean(x * x, axis=-1, keepdims=True) + EPS)
    xn = (x * factor * gain_ref[...]).astype(BF)
    xn_ref[...] = xn
    pool_ids = lax.broadcasted_iota(jnp.int32, (SLOT_ROWS, pool_ref.shape[1]), 1)
    onehot = jnp.where(idx_ref[0] == pool_ids, 1.0, 0.0).astype(BF)
    sel = mm(onehot, pool_ref[0]).astype(BF)
    sel_ref[0] = sel
    q, k, v = project(xn, sel, wq_ref[...], wk_ref[...], wv_ref[...], scale)
    q_ref[...] = q
    k_ref[0] = k
    v_ref[0] = v
    mixed = attend(q, k, v, bias_ref[0], probs_ref)
    mixed_ref[...] = mixed
    part_ref[...] = mm(mixed, wo_ref[...])


def attn_second_kernel(
    scale, x_ref, gain_ref, xn_ref, sel_ref, bias_ref, part_ref, wq_ref, wk_ref, wv_ref, wo_ref,
    q_ref, k_ref, v_ref, probs_ref, mixed_ref, middle_ref, nf_ref,
):
    q, k, v = project(xn_ref[...], sel_ref[0], wq_ref[...], wk_ref[...], wv_ref[...], scale)
    q_ref[...] = q
    k_ref[0] = k
    v_ref[0] = v
    mixed = attend(q, k, v, bias_ref[0], probs_ref)
    mixed_ref[...] = mixed
    middle = x_ref[...].astype(F32) + part_ref[...] + mm(mixed, wo_ref[...])
    middle_ref[...] = middle
    factor = lax.rsqrt(jnp.mean(middle * middle, axis=-1, keepdims=True) + EPS)
    nf_ref[...] = (middle * factor * gain_ref[...]).astype(BF)


def attention_forward(tokens, gain_attn, gain_ffn, pool, idx, bias, own, other):
    rows, width = tokens.shape
    seqs, keys = bias.shape[:2]
    length = rows // seqs
    inner = own[0].shape[1]
    heads = inner // HDIM
    scale = HDIM ** (-0.5)
    sds = jax.ShapeDtypeStruct
    qkvp = [
        (sds((rows, inner), BF), rows_of(length, inner)),
        (sds((seqs, keys, inner), BF), seq_of(keys, inner)),
        (sds((seqs, keys, inner), BF), seq_of(keys, inner)),
        (sds((seqs, heads, keys, length), BF), seq_of(heads, keys, length)),
        (sds((rows, inner), BF), rows_of(length, inner)),
    ]
    weights = [whole(w.shape) for w in own]
    flops = 2 * rows * (4 * width * inner + 2 * inner * keys)
    outs = [
        (sds((rows, width), BF), rows_of(length, width)),
        (sds((seqs, SLOT_ROWS, width), BF), seq_of(SLOT_ROWS, width)),
        *qkvp,
        (sds((rows, width), F32), rows_of(length, width)),
    ]
    xn, sel, *first, part = pl.pallas_call(
        functools.partial(attn_first_kernel, scale),
        grid=(seqs,),
        out_shape=[o[0] for o in outs],
        in_specs=[
            rows_of(length, width),
            whole((1, width)),
            seq_of(*pool.shape[1:]),
            seq_of(SLOT_ROWS, 1),
            seq_of(keys, 1),
            *weights,
        ],
        out_specs=[o[1] for o in outs],
        compiler_params=params(),
        cost_estimate=pl.CostEstimate(flops=flops, bytes_accessed=16 << 20, transcendentals=0),
        name="attn_first",
    )(tokens, gain_attn[None], pool, idx, bias, *own)
    outs = [
        *qkvp,
        (sds((rows, width), F32), rows_of(length, width)),
        (sds((rows, width), BF), rows_of(length, width)),
    ]
    *second, middle, nf = pl.pallas_call(
        functools.partial(attn_second_kernel, scale),
        grid=(seqs,),
        out_shape=[o[0] for o in outs],
        in_specs=[
            rows_of(length, width),
            whole((1, width)),
            rows_of(length, width),
            seq_of(SLOT_ROWS, width),
            seq_of(keys, 1),
            rows_of(length, width),
            *weights,
        ],
        out_specs=[o[1] for o in outs],
        compiler_params=params(),
        cost_estimate=pl.CostEstimate(flops=flops, bytes_accessed=16 << 20, transcendentals=0),
        name="attn_second",
    )(tokens, gain_ffn[None], xn, sel, bias, part, *other)
    return xn, sel, first, second, middle, nf


def gate_and_slope(h):
    c = 0.7978845608028654
    square = h * h
    t = jnp.tanh(h * (c + (c * 0.044715) * square))
    half = 0.5 + 0.5 * t
    slope = half + (0.5 * h) * (1.0 - t * t) * (c + (3.0 * c * 0.044715) * square)
    return h * half, slope


def ffn_kernel(
    first, last, chunk, nf_ref, cot_ref, wuo_ref, wut_ref, wdo_ref, wdt_ref, gain_ref,
    middle_hbm, out_hbm, dnf_hbm, *refs,
):
    if last:
        own_ref, oth_hbm, block_ref, gm_ref, gmb_ref, gg_ref = refs[:6]
    else:
        own_ref, oth_hbm, out_ref, dnf_ref = refs[:4]
    wu_s, wd_s, out_s, dnf_s, mid_s, act_s, di_s, oth_s, sems = refs[-9:]
    step = pl.program_id(0)
    rows, width = nf_ref.shape
    loads = [pltpu.make_async_copy(middle_hbm if first else out_hbm, out_s, sems.at[0])]
    if not first:
        loads.append(pltpu.make_async_copy(dnf_hbm, dnf_s, sems.at[1]))
    if last:
        loads.append(pltpu.make_async_copy(middle_hbm, mid_s, sems.at[2]))
    store = pltpu.make_async_copy(oth_s, oth_hbm, sems.at[3])

    @pl.when(step == 0)
    def _():
        for load in loads:
            load.start()
        wu_s[...] = wut_ref[...]
        wd_s[...] = wdt_ref[...]
        if first:
            dnf_s[...] = jnp.zeros_like(dnf_s)

    @pl.when(step == 1)
    def _():
        wu_s[...] = wuo_ref[...]
        wd_s[...] = wdo_ref[...]

    def inner(r, carry):
        at = pl.ds(pl.multiple_of(r * chunk, chunk), chunk)
        h = mm(nf_ref[at], wu_s[...])
        da = mm(cot_ref[at], wd_s[...], NT)
        act, slope = gate_and_slope(h)
        act_s[at] = act.astype(BF)
        di_s[at] = (da * slope).astype(BF)
        return carry

    lax.fori_loop(0, rows // chunk, inner, 0)

    @pl.when(step == 0)
    def _():
        for load in loads:
            load.wait()

    def outer(r, carry):
        at = pl.ds(pl.multiple_of(r * chunk, chunk), chunk)
        out_s[at] += mm(act_s[at], wd_s[...])
        dnf_s[at] += mm(di_s[at], wu_s[...], NT)
        return carry

    lax.fori_loop(0, rows // chunk, outer, 0)
    dwd = mm(act_s[...], cot_ref[...], TN).astype(BF)
    dwu = mm(nf_ref[...], di_s[...], TN).astype(BF)
    units = dwd.shape[0]

    @pl.when(step == 0)
    def _():
        oth_s[:units] = dwd
        oth_s[units:] = dwu
        store.start()

    @pl.when(step == 1)
    def _():
        own_ref[:units] = dwd
        own_ref[units:] = dwu
        if last:
            total = jnp.zeros((1, width), F32)
            for r in range(rows // chunk):
                at = slice(r * chunk, (r + 1) * chunk)
                block_ref[at] = out_s[at].astype(BF)
                middle, dnf = mid_s[at], dnf_s[at]
                factor = lax.rsqrt(jnp.mean(middle * middle, axis=-1, keepdims=True) + EPS)
                scaled = middle * factor
                total += jnp.sum(dnf * scaled, axis=0, keepdims=True)
                e = gain_ref[...] * dnf
                inner_mean = jnp.mean(e * scaled, axis=-1, keepdims=True)
                gm = cot_ref[at].astype(F32) + factor * (e - scaled * inner_mean)
                gm_ref[at] = gm
                gmb_ref[at] = gm.astype(BF)
            gg_ref[...] = total
        else:
            out_ref[...] = out_s[...]
            dnf_ref[...] = dnf_s[...]
        store.wait()


def ffn_part(index, count, nf, cot, wu_own, wu_oth, wd_own, wd_oth, gain_ffn, middle, out, dnf):
    rows, width = nf.shape
    units = wu_own.shape[1] // count
    first, last = index == 0, index == count - 1
    sds = jax.ShapeDtypeStruct
    grads = sds((2 * units, width), BF)
    anywhere = pl.BlockSpec(memory_space=pl.ANY)
    up = pl.BlockSpec((width, units), lambda s: (0, index))
    down = pl.BlockSpec((units, width), lambda s: (index, 0))
    full = whole((rows, width))
    outs = [(grads, whole((2 * units, width))), (grads, anywhere)]
    if last:
        outs += [
            (sds((rows, width), BF), full),
            (sds((rows, width), F32), full),
            (sds((rows, width), BF), full),
            (sds((1, width), F32), whole((1, width))),
        ]
    else:
        outs += [(sds((rows, width), F32), full)] * 2
    return pl.pallas_call(
        functools.partial(ffn_kernel, first, last, 256),
        grid=(2,),
        out_shape=[o[0] for o in outs],
        in_specs=[full, full, up, up, down, down, whole((1, width)), anywhere, anywhere, anywhere],
        out_specs=[o[1] for o in outs],
        scratch_shapes=[
            pltpu.VMEM((width, units), BF),
            pltpu.VMEM((units, width), BF),
            pltpu.VMEM((rows, width), F32),
            pltpu.VMEM((rows, width), F32),
            pltpu.VMEM((rows, width) if last else (8, 128), F32),
            pltpu.VMEM((rows, units), BF),
            pltpu.VMEM((rows, units), BF),
            pltpu.VMEM((2 * units, width), BF),
            pltpu.SemaphoreType.DMA((4,)),
        ],
        compiler_params=params(),
        cost_estimate=pl.CostEstimate(
            flops=24 * rows * width * units, bytes_accessed=24 << 20, transcendentals=0
        ),
        name="ffn_part",
    )(nf, cot, wu_own, wu_oth, wd_own, wd_oth, gain_ffn[None], middle, out, dnf)


def stack_halves(grad):
    half = grad.shape[0] // 2
    return jnp.concatenate([grad[:half], grad[half:]], axis=1)


def mix_back_kernel(
    length, gm_ref, xn_ref, sel_ref, selall_ref, woo_ref, wot_ref, po_ref, pt_ref, mo_ref, mt_ref,
    dmo_ref, dmt_ref, dvo_ref, dvt_ref, own_ref, oth_ref,
    awoo, awot, awvo, awvt, slo, slt,
):
    step = pl.program_id(0)
    masks = head_masks()
    gm = gm_ref[...]
    xn = xn_ref[...]

    @pl.when(step == 0)
    def _():
        for acc in (awoo, awot, awvo, awvt):
            acc[...] = jnp.zeros_like(acc)

    for wo_ref, p_ref, m_ref, dm_ref, dv_ref, awo, awv, sl in (
        (woo_ref, po_ref, mo_ref, dmo_ref, dvo_ref, awoo, awvo, slo),
        (wot_ref, pt_ref, mt_ref, dmt_ref, dvt_ref, awot, awvt, slt),
    ):
        awo[...] += mm(m_ref[...], gm, TN)
        dmix = mm(gm, wo_ref[...], NT).astype(BF)
        dm_ref[...] = dmix
        pieces = []
        for pair in range(dmix.shape[1] // (2 * HDIM)):
            dp = dmix[:, pair * 2 * HDIM : (pair + 1) * 2 * HDIM]
            dv = None
            for half, mask in enumerate(masks):
                part = mm(p_ref[0, 2 * pair + half], jnp.where(mask, dp, 0))
                dv = part if dv is None else dv + part
            pieces.append(dv.astype(BF))
        dv = jnp.concatenate(pieces, axis=1)
        dv_ref[0] = dv
        awv[...] += mm(xn, dv[:length], TN)
        sl[pl.ds(pl.multiple_of(step * SLOT_ROWS, SLOT_ROWS), SLOT_ROWS)] = dv[length:]

    @pl.when(step == pl.num_programs(0) - 1)
    def _():
        for ref, awo, awv, sl in ((own_ref, awoo, awvo, slo), (oth_ref, awot, awvt, slt)):
            inner = awo.shape[0]
            ref[:inner] = awo[...].astype(BF)
            ref[inner:] = stack_halves((awv[...] + mm(selall_ref[...], sl[...], TN)).astype(BF))


def mix_back(gmb, xn, sel, wo_own, wo_oth, own, oth):
    rows, width = gmb.shape
    seqs, heads, keys, length = own[3].shape
    inner = wo_own.shape[0]
    sds = jax.ShapeDtypeStruct
    row, head = rows_of(length, width), rows_of(length, inner)
    probs = seq_of(heads, keys, length)
    grads = sds((2 * inner, width), BF)
    outs = [
        (sds((rows, inner), BF), head),
        (sds((rows, inner), BF), head),
        (sds((seqs, keys, inner), BF), seq_of(keys, inner)),
        (sds((seqs, keys, inner), BF), seq_of(keys, inner)),
        (grads, whole(grads.shape)),
        (grads, whole(grads.shape)),
    ]
    return pl.pallas_call(
        functools.partial(mix_back_kernel, length),
        grid=(seqs,),
        out_shape=[o[0] for o in outs],
        in_specs=[
            row, row, seq_of(SLOT_ROWS, width), whole((seqs * SLOT_ROWS, width)),
            whole((inner, width)), whole((inner, width)), probs, probs, head, head,
        ],
        out_specs=[o[1] for o in outs],
        scratch_shapes=[
            pltpu.VMEM((inner, width), F32),
            pltpu.VMEM((inner, width), F32),
            pltpu.VMEM((width, inner), F32),
            pltpu.VMEM((width, inner), F32),
            pltpu.VMEM((seqs * SLOT_ROWS, inner), BF),
            pltpu.VMEM((seqs * SLOT_ROWS, inner), BF),
        ],
        compiler_params=params(),
        cost_estimate=pl.CostEstimate(
            flops=14 * rows * width * inner, bytes_accessed=20 << 20, transcendentals=0
        ),
        name="mix_back",
    )(gmb, xn, sel, sel.reshape(seqs * SLOT_ROWS, width), wo_own, wo_oth, own[3], oth[3], own[4], oth[4])


def score_back_kernel(
    length, scale, xn_ref, selall_ref, qo_ref, qt_ref, ko_ref, kt_ref, vo_ref, vt_ref,
    po_ref, pt_ref, dmo_ref, dmt_ref,
    dqo_ref, dqt_ref, dko_ref, dkt_ref, own_ref, oth_ref,
    awqo, awqt, awko, awkt, slo, slt,
):
    step = pl.program_id(0)
    masks = head_masks()
    xn = xn_ref[...]

    @pl.when(step == 0)
    def _():
        for acc in (awqo, awqt, awko, awkt):
            acc[...] = jnp.zeros_like(acc)

    for q_ref, k_ref, v_ref, p_ref, dm_ref, dq_ref, dk_ref, awq, awk, sl in (
        (qo_ref, ko_ref, vo_ref, po_ref, dmo_ref, dqo_ref, dko_ref, awqo, awko, slo),
        (qt_ref, kt_ref, vt_ref, pt_ref, dmt_ref, dqt_ref, dkt_ref, awqt, awkt, slt),
    ):
        dqs, dks = [], []
        for pair in range(q_ref.shape[1] // (2 * HDIM)):
            cols = slice(pair * 2 * HDIM, (pair + 1) * 2 * HDIM)
            qp, kp, vp, dp = q_ref[:, cols], k_ref[0, :, cols], v_ref[0, :, cols], dm_ref[:, cols]
            dq = dk = None
            for half, mask in enumerate(masks):
                probs = p_ref[0, 2 * pair + half].astype(F32)
                weighted = mm(vp, jnp.where(mask, dp, 0), NT)
                delta = jnp.sum(probs * weighted, axis=0, keepdims=True)
                ds = (probs * (weighted - delta)).astype(BF)
                dq_part = mm(ds, jnp.where(mask, kp, 0), TN)
                dk_part = mm(ds, jnp.where(mask, qp, 0))
                dq = dq_part if dq is None else dq + dq_part
                dk = dk_part if dk is None else dk + dk_part
            dqs.append((dq * scale).astype(BF))
            dks.append(dk.astype(BF))
        dq = jnp.concatenate(dqs, axis=1)
        dk = jnp.concatenate(dks, axis=1)
        dq_ref[...] = dq
        dk_ref[0] = dk
        awq[...] += mm(xn, dq, TN)
        awk[...] += mm(xn, dk[:length], TN)
        sl[pl.ds(pl.multiple_of(step * SLOT_ROWS, SLOT_ROWS), SLOT_ROWS)] = dk[length:]

    @pl.when(step == pl.num_programs(0) - 1)
    def _():
        for ref, awq, awk, sl in ((own_ref, awqo, awko, slo), (oth_ref, awqt, awkt, slt)):
            half = awq.shape[0] // 2
            ref[:half] = stack_halves(awq[...].astype(BF))
            ref[half:] = stack_halves((awk[...] + mm(selall_ref[...], sl[...], TN)).astype(BF))


def score_back(xn, sel, own, oth, dm_own, dm_oth):
    rows, width = xn.shape
    seqs, heads, keys, length = own[3].shape
    inner = dm_own.shape[1]
    sds = jax.ShapeDtypeStruct
    head, key = rows_of(length, inner), seq_of(keys, inner)
    probs = seq_of(heads, keys, length)
    grads = sds((width, 2 * inner), BF)
    outs = [
        (sds((rows, inner), BF), head),
        (sds((rows, inner), BF), head),
        (sds((seqs, keys, inner), BF), key),
        (sds((seqs, keys, inner), BF), key),
        (grads, whole(grads.shape)),
        (grads, whole(grads.shape)),
    ]
    return pl.pallas_call(
        functools.partial(score_back_kernel, length, HDIM ** (-0.5)),
        grid=(seqs,),
        out_shape=[o[0] for o in outs],
        in_specs=[
            rows_of(length, width), whole((seqs * SLOT_ROWS, width)),
            head, head, key, key, key, key, probs, probs, head, head,
        ],
        out_specs=[o[1] for o in outs],
        scratch_shapes=[
            pltpu.VMEM((width, inner), F32),
            pltpu.VMEM((width, inner), F32),
            pltpu.VMEM((width, inner), F32),
            pltpu.VMEM((width, inner), F32),
            pltpu.VMEM((seqs * SLOT_ROWS, inner), BF),
            pltpu.VMEM((seqs * SLOT_ROWS, inner), BF),
        ],
        compiler_params=params(),
        cost_estimate=pl.CostEstimate(
            flops=18 * rows * width * inner, bytes_accessed=20 << 20, transcendentals=0
        ),
        name="score_back",
    )(
        xn, sel.reshape(seqs * SLOT_ROWS, width), own[0], oth[0], own[1], oth[1], own[2], oth[2],
        own[3], oth[3], dm_own, dm_oth,
    )


def input_back_kernel(
    length, x_ref, gm_ref, gain_ref, idx_ref, wqo, wqt, wko, wkt, wvo, wvt,
    dqo, dqt, dko, dkt, dvo, dvt, gx_ref, gp_ref, gg_ref,
):
    def both(own, oth, axis):
        return jnp.concatenate([own, oth], axis=axis)

    dkeys = mm(both(dko[0], dkt[0], 1), both(wko[...], wkt[...], 1), NT)
    dkeys += mm(both(dvo[0], dvt[0], 1), both(wvo[...], wvt[...], 1), NT)
    dxn = dkeys[:length] + mm(both(dqo[...], dqt[...], 1), both(wqo[...], wqt[...], 1), NT)
    x = x_ref[...].astype(F32)
    factor = lax.rsqrt(jnp.mean(x * x, axis=-1, keepdims=True) + EPS)
    scaled = x * factor
    c = gain_ref[...] * dxn
    inner_mean = jnp.mean(c * scaled, axis=-1, keepdims=True)
    gx_ref[...] = gm_ref[...] + factor * (c - scaled * inner_mean)
    total = jnp.sum(dxn * scaled, axis=0, keepdims=True)
    first = pl.program_id(0) == 0
    gg_ref[...] = jnp.where(first, 0.0, gg_ref[...]) + total
    pool_ids = lax.broadcasted_iota(jnp.int32, (SLOT_ROWS, gp_ref.shape[1]), 1)
    onehot = jnp.where(idx_ref[0] == pool_ids, 1.0, 0.0).astype(BF)
    gp_ref[0] = mm(onehot, dkeys[length:].astype(BF), TN)


def input_back(tokens, gm, gain_attn, idx, pool_rows, own, oth, dq, dk, dv):
    rows, width = tokens.shape
    seqs, keys, inner = dk[0].shape
    length = rows // seqs
    sds = jax.ShapeDtypeStruct
    row, head, key = rows_of(length, width), rows_of(length, inner), seq_of(keys, inner)
    return pl.pallas_call(
        functools.partial(input_back_kernel, length),
        grid=(seqs,),
        out_shape=[
            sds((rows, width), F32),
            sds((seqs, pool_rows, width), F32),
            sds((1, width), F32),
        ],
        in_specs=[
            row, row, whole((1, width)), seq_of(SLOT_ROWS, 1), *[whole((width, inner))] * 6,
            head, head, key, key, key, key,
        ],
        out_specs=[row, seq_of(pool_rows, width), whole((1, width))],
        compiler_params=params(),
        cost_estimate=pl.CostEstimate(
            flops=12 * rows * width * inner, bytes_accessed=20 << 20, transcendentals=0
        ),
        name="input_back",
    )(
        tokens, gm, gain_attn[None], idx, own[0], oth[0], own[1], oth[1], own[2], oth[2],
        *dq, *dk, *dv,
    )


class ChipSum:
    def __init__(self, dp, mp):
        bits = dp.bit_length() - 1
        here = lax.axis_index("dp")
        second = lax.axis_index("mp") % 2 == 1
        masks = [1 << b for b in range(bits)]
        sides = [(here >> b) & 1 for b in range(bits)]
        if bits == 4:
            masks[3] = 12
            sides[2] = sides[2] ^ sides[3]
        swapped = list(masks)
        if bits > 1:
            swapped[0], swapped[1] = masks[1], masks[0]
            sides[0], sides[1] = (
                jnp.where(second, sides[1], sides[0]),
                jnp.where(second, sides[0], sides[1]),
            )
        self.sides = sides
        self.pairs = [
            [
                (d * mp + m, (d ^ (swapped if m % 2 else masks)[b]) * mp + m)
                for d in range(dp)
                for m in range(mp)
            ]
            for b in range(bits)
        ]

    def exchange(self, step, array):
        return lax.ppermute(array, ("dp", "mp"), self.pairs[step])

    def reduce(self, parts):
        for step, side in enumerate(self.sides):
            halves = [p.reshape(2, p.shape[0] // 2, p.shape[1]) for p in parts]

            def pick(at):
                return sum(
                    lax.dynamic_index_in_dim(h, at, 0, keepdims=False).astype(F32) for h in halves
                ).astype(BF)

            sent = self.exchange(step, pick(1 - side))
            parts = [pick(side), sent]
        return (parts[0].astype(F32) + parts[1].astype(F32)).astype(BF)

    def gather(self, piece):
        for step in reversed(range(len(self.sides))):
            got = self.exchange(step, piece)
            side = self.sides[step] == 1
            piece = jnp.concatenate(
                [jnp.where(side, got, piece), jnp.where(side, piece, got)], axis=0
            )
        return piece


def body(
    dp, mp, tokens, cotangent, w_query, key_projection_weight, value_projection_weight, w_out,
    w_up, w_down, gain_attn, gain_ffn, value_pool, slot_index, slot_count, pad_mask,
):
    length = pad_mask.shape[1]
    slots = slot_index.shape[1]
    seqs = tokens.shape[0] // length
    mine = lax.axis_index("mp") * seqs

    def core_swap(array):
        return lax.ppermute(array, "mp", [(i, i ^ 1) for i in range(mp)])

    def local(array):
        return lax.dynamic_slice_in_dim(array, mine, seqs, 0)

    own = (w_query, key_projection_weight, value_projection_weight, w_out)
    oth = tuple(core_swap(w) for w in own)
    wu_oth, wd_oth = core_swap(w_up), core_swap(w_down)

    pool, index = local(value_pool), local(slot_index)
    counts, pads = local(slot_count), local(pad_mask)
    index = jnp.pad(index, ((0, 0), (0, SLOT_ROWS - slots)), constant_values=-1)[:, :, None]
    slot_ids = lax.broadcasted_iota(jnp.int32, (1, SLOT_ROWS), 1)
    valid = jnp.concatenate([pads > 0, slot_ids < counts[:, None]], axis=1)
    bias = jnp.where(valid, 0.0, -1e9).astype(F32)[:, :, None]

    xn, sel, first, second, middle, nf = attention_forward(
        tokens, gain_attn, gain_ffn, pool, index, bias, own, oth
    )
    weights = (w_up, wu_oth, w_down, wd_oth)
    f0_own, f0_oth, out, dnf = ffn_part(
        0, 2, nf, cotangent, *weights, gain_ffn, middle, middle, middle
    )
    chips = ChipSum(dp, mp)

    def total(grad_own, grad_oth):
        return chips.gather(chips.reduce([grad_own, core_swap(grad_oth)]))

    sum0 = total(f0_own, f0_oth)
    f1_own, f1_oth, block_out, gm, gmb, gg_ffn = ffn_part(
        1, 2, nf, cotangent, *weights, gain_ffn, middle, out, dnf
    )
    sum1 = total(f1_own, f1_oth)
    dm_own, dm_oth, dv_own, dv_oth, a0_own, a0_oth = mix_back(
        gmb, xn, sel, w_out, oth[3], first, second
    )
    sum2 = total(a0_own, a0_oth)
    dq_own, dq_oth, dk_own, dk_oth, a1_own, a1_oth = score_back(
        xn, sel, first, second, dm_own, dm_oth
    )
    sum3 = total(a1_own, a1_oth)
    grad_tokens, grad_pool, gg_attn = input_back(
        tokens, gm, gain_attn, index, value_pool.shape[1], own, oth,
        (dq_own, dq_oth), (dk_own, dk_oth), (dv_own, dv_oth),
    )
    gains = lax.psum(jnp.concatenate([gg_attn, gg_ffn], axis=0), ("dp", "mp"))
    peer_pool = core_swap(grad_pool)
    is_first = lax.axis_index("mp") == 0
    grad_value_pool = jnp.concatenate(
        [
            jnp.where(is_first, grad_pool, peer_pool),
            jnp.where(is_first, peer_pool, grad_pool),
        ],
        axis=0,
    )
    units = w_up.shape[1] // 2
    inner = w_out.shape[0]

    def unstack(block):
        return jnp.concatenate([block[:, :inner], block[:, inner:]], axis=0).astype(F32)

    return (
        block_out,
        grad_tokens,
        unstack(sum3[:inner]),
        unstack(sum3[inner:]),
        unstack(sum2[inner:]),
        sum2[:inner].astype(F32),
        jnp.concatenate([sum0[units:], sum1[units:]], axis=1).astype(F32),
        jnp.concatenate([sum0[:units], sum1[:units]], axis=0).astype(F32),
        gains[0],
        gains[1],
        grad_value_pool,
    )


def solution(mesh):
    placed = (
        P(("dp", "mp"), None),
        P(("dp", "mp"), None),
        P(None, "mp"),
        P(None, "mp"),
        P(None, "mp"),
        P("mp", None),
        P(None, "mp"),
        P("mp", None),
        P(),
        P(),
        P("dp", None, None),
        P("dp", None),
        P("dp"),
        P("dp", None),
    )
    return jax.shard_map(
        functools.partial(body, mesh.shape["dp"], mesh.shape["mp"]),
        mesh=mesh,
        in_specs=placed,
        out_specs=(
            P(("dp", "mp"), None),
            P(("dp", "mp"), None),
            P(None, "mp"),
            P(None, "mp"),
            P(None, "mp"),
            P("mp", None),
            P(None, "mp"),
            P("mp", None),
            P(),
            P(),
            P("dp", None, None),
        ),
        check_vma=False,
    )
```

```python
import functools

import jax
import jax.numpy as jnp
from jax import lax
from jax.experimental import pallas as pl
from jax.experimental.pallas import tpu as pltpu
from jax.sharding import PartitionSpec as P

HDIM = 64
SCALE = HDIM ** (-0.5)
EPS = 1e-06
SLOT_ROWS = 32
BF = jnp.bfloat16
F32 = jnp.float32
MIB = 1 << 20

NN = (((1,), (0,)), ((), ()))
NT = (((1,), (1,)), ((), ()))
TN = (((0,), (0,)), ((), ()))
ANYWHERE = pl.BlockSpec(memory_space=pl.ANY)
IN_SMEM = pl.BlockSpec(memory_space=pltpu.SMEM)
sds = jax.ShapeDtypeStruct


def mm(left, right, dims=NN):
    return lax.dot_general(left, right, dims, preferred_element_type=F32)


def params(mib):
    return pltpu.CompilerParams(vmem_limit_bytes=mib * MIB)


def cost(us):
    return pl.CostEstimate(flops=int(us * 1.15e9), bytes_accessed=0, transcendentals=0)


def stored(shape, dtype):
    return pltpu.HBM(shape, dtype)


def streamed(*arrays):
    return [pltpu.with_memory_space_constraint(a, pltpu.HBM) for a in arrays]


def whole(shape):
    zeros = (0,) * len(shape)
    return pl.BlockSpec(shape, lambda *_: zeros)


def rows_of(rows, width):
    return pl.BlockSpec((rows, width), lambda s, *_: (s, 0))


def seq_of(*shape):
    tail = (0,) * len(shape)
    return pl.BlockSpec((1, *shape), lambda s, *_: (s, *tail))


MARK = sds((8, 128), F32)
MARK_SPEC = whole((8, 128))


def marked(refs):
    refs[-1][...] = jnp.zeros_like(refs[-1])
    return refs[:-1]


def head_masks():
    lanes = lax.broadcasted_iota(jnp.int32, (1, 2 * HDIM), 1)
    return lanes < HDIM, lanes >= HDIM


def pair_columns(width):
    return [slice(at, at + 2 * HDIM) for at in range(0, width, 2 * HDIM)]


def attend(q, k, v, bias, probs_ref):
    masks = head_masks()
    pieces = []
    for pair, cols in enumerate(pair_columns(q.shape[1])):
        qp, kp, vp = q[:, cols], k[:, cols], v[:, cols]
        mixed = None
        for half, mask in enumerate(masks):
            scores = mm(kp, jnp.where(mask, qp, 0), NT) + bias
            peak = jnp.max(scores, axis=0, keepdims=True)
            raised = jnp.exp(scores - peak)
            total = jnp.sum(raised, axis=0, keepdims=True)
            probs = (raised * (1.0 / total)).astype(BF)
            probs_ref[0, 2 * pair + half] = probs
            part = mm(probs, jnp.where(mask, vp, 0), TN)
            mixed = part if mixed is None else mixed + part
        pieces.append(mixed.astype(BF))
    return jnp.concatenate(pieces, axis=1)


def project(xn, sel, wq, wk, wv):
    rows = jnp.concatenate([xn, sel], axis=0)
    q = (mm(xn, wq) * SCALE).astype(BF)
    k = mm(rows, wk).astype(BF)
    v = mm(rows, wv).astype(BF)
    return q, k, v


def key_bias(seq, counts_ref, pads_ref, length):
    tokens = jnp.sum(pads_ref[pl.ds(seq, 1), :], axis=1, keepdims=True)
    token_ids = lax.broadcasted_iota(jnp.int32, (length, 1), 0)
    slot_ids = lax.broadcasted_iota(jnp.int32, (SLOT_ROWS, 1), 0)
    live = jnp.concatenate([token_ids < tokens, slot_ids < counts_ref[seq]], axis=0)
    return jnp.where(live, 0.0, -1e9).astype(F32)


def attn_first_kernel(
    first_ref, counts_ref, idx_ref, x_ref, gain_ref, pool_ref, pads_ref, wq_ref, wk_ref, wv_ref,
    xn_ref, sel_ref, bias_ref, hot_ref, q_ref, k_ref, v_ref, probs_ref, mixed_ref,
):
    seq = first_ref[0] + pl.program_id(0)
    x = x_ref[...].astype(F32)
    factor = lax.rsqrt(jnp.mean(x * x, axis=-1, keepdims=True) + EPS)
    xn = (x * factor * gain_ref[...].reshape(1, -1)).astype(BF)
    xn_ref[...] = xn
    spots = (pool_ref.shape[1], SLOT_ROWS)
    pool_ids = lax.broadcasted_iota(jnp.int32, spots, 0)
    slot_ids = lax.broadcasted_iota(jnp.int32, spots, 1)
    chosen = jnp.full(spots, -1, jnp.int32)
    for slot in range(idx_ref.shape[1]):
        chosen = jnp.where(slot_ids == slot, idx_ref[seq, slot], chosen)
    hot = jnp.where(chosen == pool_ids, 1.0, 0.0).astype(BF)
    hot_ref[0] = hot
    sel = mm(hot, pool_ref[0], TN).astype(BF)
    sel_ref[0] = sel
    bias = key_bias(seq, counts_ref, pads_ref, x_ref.shape[0])
    bias_ref[0] = bias
    q, k, v = project(xn, sel, wq_ref[...], wk_ref[...], wv_ref[...])
    q_ref[...] = q
    k_ref[0] = k
    v_ref[0] = v
    mixed_ref[...] = attend(q, k, v, bias, probs_ref)


def attn_second_kernel(
    x_ref, gain_ref, xn_ref, sel_ref, bias_ref, first_ref, wq_ref, wk_ref, wv_ref, woo_ref, wot_ref,
    q_ref, k_ref, v_ref, probs_ref, mixed_ref, middle_ref, nf_ref,
):
    q, k, v = project(xn_ref[...], sel_ref[0], wq_ref[...], wk_ref[...], wv_ref[...])
    q_ref[...] = q
    k_ref[0] = k
    v_ref[0] = v
    mixed = attend(q, k, v, bias_ref[0], probs_ref)
    mixed_ref[...] = mixed
    middle = x_ref[...].astype(F32) + mm(first_ref[...], woo_ref[...]) + mm(mixed, wot_ref[...])
    middle_ref[...] = middle
    factor = lax.rsqrt(jnp.mean(middle * middle, axis=-1, keepdims=True) + EPS)
    nf_ref[...] = (middle * factor * gain_ref[...].reshape(1, -1)).astype(BF)


def attention_forward(tokens, gain_attn, gain_ffn, pool, idx, counts, pads, seqs, mine, own, other):
    rows, width = tokens.shape
    length = rows // seqs
    keys = length + SLOT_ROWS
    inner = own[0].shape[1]
    heads = inner // HDIM
    row, head, key = rows_of(length, width), rows_of(length, inner), seq_of(keys, inner)
    kept = [
        (stored((rows, inner), BF), head),
        (stored((seqs, keys, inner), BF), key),
        (stored((seqs, keys, inner), BF), key),
        (stored((seqs, heads, keys, length), BF), seq_of(heads, keys, length)),
        (stored((rows, inner), BF), head),
    ]
    weight = whole((width, inner))
    outs = [
        (stored((rows, width), BF), row),
        (stored((seqs, SLOT_ROWS, width), BF), seq_of(SLOT_ROWS, width)),
        (stored((seqs, keys, 1), F32), seq_of(keys, 1)),
        (stored((seqs, pool.shape[1], SLOT_ROWS), BF), seq_of(pool.shape[1], SLOT_ROWS)),
        *kept,
    ]
    xn, sel, bias, hot, *first = pl.pallas_call(
        attn_first_kernel,
        grid_spec=pltpu.PrefetchScalarGridSpec(
            num_scalar_prefetch=3,
            grid=(seqs,),
            in_specs=[
                row,
                whole((width,)),
                pl.BlockSpec((1, *pool.shape[1:]), lambda s, first, *_: (first[0] + s, 0, 0)),
                whole(pads.shape),
                weight, weight, weight,
            ],
            out_specs=[o[1] for o in outs],
        ),
        out_shape=[o[0] for o in outs],
        compiler_params=params(14),
        cost_estimate=cost(12),
        name="attn_first",
    )(mine, counts, idx, *streamed(tokens, gain_attn, pool, pads, *own[:3]))
    outs = [
        *kept,
        (stored((rows, width), F32), row),
        (stored((rows, width), BF), row),
    ]
    *second, middle, nf = pl.pallas_call(
        attn_second_kernel,
        grid=(seqs,),
        out_shape=[o[0] for o in outs],
        in_specs=[
            row,
            whole((width,)),
            row,
            seq_of(SLOT_ROWS, width),
            seq_of(keys, 1),
            head,
            weight, weight, weight,
            whole((inner, width)),
            whole((inner, width)),
        ],
        out_specs=[o[1] for o in outs],
        compiler_params=params(18),
        cost_estimate=cost(12),
        name="attn_second",
    )(
        *streamed(tokens, gain_ffn),
        *streamed(xn, sel, bias, first[4]),
        *other[:3], *streamed(own[3]), other[3],
    )
    return xn, sel, hot, first, second, middle, nf


def gate_and_slope(h):
    c = 0.7978845608028654
    square = h * h
    t = jnp.tanh(h * (c + (c * 0.044715) * square))
    half = 0.5 + 0.5 * t
    slope = half + (0.5 * h) * (1.0 - t * t) * (c + (3.0 * c * 0.044715) * square)
    return h * half, slope


def ffn_kernel(own, chunk, nf_ref, cot_ref, wu_ref, wd_ref, *refs):
    rows = nf_ref.shape[0]
    units = wu_ref.shape[1]
    if own:
        got_ref, sides_ref = refs[:2]
        act_ref, di_ref, keep_ref, send_ref = marked(refs)[-4:]
    else:
        act_ref, di_ref, grad_ref = marked(refs)[-3:]
    wu, wd = wu_ref[...], wd_ref[...]
    for r in range(rows // chunk):
        at = slice(r * chunk, (r + 1) * chunk)
        act, slope = gate_and_slope(mm(nf_ref[at], wu))
        act_ref[at] = act.astype(BF)
        di_ref[at] = (mm(cot_ref[at], wd, NT) * slope).astype(BF)
    at = pl.ds(pl.multiple_of(pl.program_id(0) * units, units), units)
    down = mm(act_ref[...], cot_ref[...], TN).astype(BF)
    up = mm(nf_ref[...], di_ref[...], TN).astype(BF)
    if not own:
        grad_ref[0, at] = down
        grad_ref[1, :, at] = up
        return
    down = bf_sum(down, got_ref[0, at])
    up = bf_sum(up, got_ref[1, :, at])
    upper = sides_ref[0] == 1

    @pl.when(upper)
    def _():
        keep_ref[:, at] = up
        send_ref[at] = down

    @pl.when(jnp.logical_not(upper))
    def _():
        keep_ref[at] = down
        send_ref[:, at] = up


def ffn_part(index, nf, cot, weights, sums=(), after=()):
    rows, width = nf.shape
    own = len(sums) > 0
    units = 256
    steps = width // units
    full, square, part = whole((rows, width)), (width, width), pl.BlockSpec((rows, units), lambda j: (0, j))
    grads = [sds(square, BF)] * 2 if own else [sds((2, *square), BF)]
    extra = [whole((2, *square)), IN_SMEM] if own else []
    return pl.pallas_call(
        functools.partial(ffn_kernel, own, 256),
        grid=(steps,),
        out_shape=[*[stored((rows, width), BF)] * 2, *grads, MARK],
        in_specs=[
            full,
            full,
            pl.BlockSpec((width, units), lambda j: (0, index * steps + j)),
            pl.BlockSpec((units, width), lambda j: (index * steps + j, 0)),
            *extra,
            *[ANYWHERE] * len(after),
        ],
        out_specs=[part, part, *[whole(g.shape) for g in grads], MARK_SPEC],
        compiler_params=params(26),
        cost_estimate=cost(10),
        name="ffn_part",
    )(*streamed(nf, cot), *weights, *sums, *after)


def norm_back_kernel(cot_ref, middle_ref, gain_ref, wut_ref, wuo_ref, d0t, d0o, d1t, d1o, *refs):
    gm_ref, gmb_ref, gg_ref = marked(refs)[-3:]
    middle = middle_ref[...]
    width = middle.shape[1]
    dnf = 0.0
    for at, parts in enumerate(((d0t, d0o), (d1t, d1o))):
        cols = slice(at * width, (at + 1) * width)
        for part, wu_ref in zip(parts, (wut_ref, wuo_ref)):
            dnf += mm(part[...], wu_ref[:, cols], NT)
    factor = lax.rsqrt(jnp.mean(middle * middle, axis=-1, keepdims=True) + EPS)
    scaled = middle * factor
    e = gain_ref[...].reshape(1, -1) * dnf
    inner_mean = jnp.mean(e * scaled, axis=-1, keepdims=True)
    gm = cot_ref[...].astype(F32) + factor * (e - scaled * inner_mean)
    gm_ref[...] = gm
    gmb_ref[...] = gm.astype(BF)
    total = jnp.sum(dnf * scaled, axis=0, keepdims=True)
    gg_ref[...] = jnp.where(pl.program_id(0) == 0, 0.0, gg_ref[...]) + total


def norm_back(cot, middle, gain_ffn, wu_oth, wu_own, dis, after=()):
    rows, width = cot.shape
    block = 256
    row = rows_of(block, width)
    return pl.pallas_call(
        norm_back_kernel,
        grid=(rows // block,),
        out_shape=[stored((rows, width), F32), stored((rows, width), BF), sds((1, width), F32), MARK],
        in_specs=[
            row, row, whole((width,)), whole(wu_own.shape), whole(wu_own.shape), row, row, row, row,
            *[ANYWHERE] * len(after),
        ],
        out_specs=[row, row, whole((1, width)), MARK_SPEC],
        compiler_params=params(22),
        cost_estimate=cost(9),
        name="norm_back",
    )(*streamed(cot, middle, gain_ffn), wu_oth, *streamed(wu_own, *dis), *after)


def block_out_kernel(middle_ref, wdt_ref, wdo_ref, a0t, a0o, a1t, a1o, *refs):
    total = middle_ref[...]
    width = total.shape[1]
    for at, parts in enumerate(((a0t, a0o), (a1t, a1o))):
        for part, wd_ref in zip(parts, (wdt_ref, wdo_ref)):
            total += mm(part[...], wd_ref[at * width : (at + 1) * width])
    marked(refs)[-1][...] = total.astype(BF)


def block_output(middle, wd_oth, wd_own, acts, after=()):
    rows, width = middle.shape
    block = 256
    row = rows_of(block, width)
    return pl.pallas_call(
        block_out_kernel,
        grid=(rows // block,),
        out_shape=[stored((rows, width), BF), MARK],
        in_specs=[
            row, whole(wd_own.shape), whole(wd_own.shape), row, row, row, row, *[ANYWHERE] * len(after),
        ],
        out_specs=[row, MARK_SPEC],
        compiler_params=params(18),
        cost_estimate=cost(8),
        name="block_out",
    )(*streamed(middle), wd_oth, *streamed(wd_own, *acts), *after)


def stack_halves(grad):
    half = grad.shape[0] // 2
    return jnp.concatenate([grad[:half], grad[half:]], axis=1)


def attn_back_kernel(
    gm_ref, xn_ref, selall_ref, wo_ref, q_ref, k_ref, v_ref, p_ref, m_ref, *refs
):
    awo, aw, slots = refs[-3:]
    dq_ref, dk_ref, dv_ref, grad_ref = marked(refs[:-3])[-4:]
    step = pl.program_id(0)
    masks = head_masks()
    gm, xn = gm_ref[...], xn_ref[...]
    length = gm.shape[0]

    @pl.when(step == 0)
    def _():
        awo[...] = jnp.zeros_like(awo)
        aw[...] = jnp.zeros_like(aw)

    awo[...] += mm(m_ref[...], gm, TN)
    dmix = mm(gm, wo_ref[...], NT).astype(BF)
    dqs, dks, dvs = [], [], []
    for pair, cols in enumerate(pair_columns(dmix.shape[1])):
        qp, kp, vp, dp = q_ref[:, cols], k_ref[0, :, cols], v_ref[0, :, cols], dmix[:, cols]
        dq = dk = dv = 0.0
        for half, mask in enumerate(masks):
            probs = p_ref[0, 2 * pair + half]
            dp_head = jnp.where(mask, dp, 0)
            weighted = mm(vp, dp_head, NT)
            high = probs.astype(F32)
            delta = jnp.sum(high * weighted, axis=0, keepdims=True)
            ds = (high * (weighted - delta)).astype(BF)
            dv += mm(probs, dp_head)
            dq += mm(ds, jnp.where(mask, kp, 0), TN)
            dk += mm(ds, jnp.where(mask, qp, 0))
        dqs.append((dq * SCALE).astype(BF))
        dks.append(dk.astype(BF))
        dvs.append(dv.astype(BF))
    dq, dk, dv = [jnp.concatenate(d, axis=1) for d in (dqs, dks, dvs)]
    dq_ref[...] = dq
    dk_ref[0] = dk
    dv_ref[0] = dv
    aw[...] += mm(xn, jnp.concatenate([dq, dk[:length], dv[:length]], axis=1), TN)
    at = pl.ds(pl.multiple_of(step * SLOT_ROWS, SLOT_ROWS), SLOT_ROWS)
    slots[at] = jnp.concatenate([dk[length:], dv[length:]], axis=1)

    @pl.when(step == pl.num_programs(0) - 1)
    def _():
        inner = awo.shape[0]
        grad_ref[:inner] = awo[...].astype(BF)
        grad_ref[inner : 2 * inner] = stack_halves(aw[:, :inner].astype(BF))
        rest = (aw[:, inner:] + mm(selall_ref[...], slots[...], TN)).astype(BF)
        grad_ref[2 * inner : 3 * inner] = stack_halves(rest[:, :inner])
        grad_ref[3 * inner :] = stack_halves(rest[:, inner:])


def attn_back(gmb, xn, sel, wo, kept, us, after=()):
    rows, width = gmb.shape
    seqs, heads, keys, length = kept[3].shape
    inner = wo.shape[0]
    row, head, key = rows_of(length, width), rows_of(length, inner), seq_of(keys, inner)
    grads = sds((4 * inner, width), BF)
    outs = [
        (stored((rows, inner), BF), head),
        (stored((seqs, keys, inner), BF), key),
        (stored((seqs, keys, inner), BF), key),
        (grads, whole(grads.shape)),
        (MARK, MARK_SPEC),
    ]
    return pl.pallas_call(
        attn_back_kernel,
        grid=(seqs,),
        out_shape=[o[0] for o in outs],
        in_specs=[
            row, row, whole((seqs * SLOT_ROWS, width)), whole((inner, width)),
            head, key, key, seq_of(heads, keys, length), head, *[ANYWHERE] * len(after),
        ],
        out_specs=[o[1] for o in outs],
        scratch_shapes=[
            pltpu.VMEM((inner, width), F32),
            pltpu.VMEM((width, 3 * inner), F32),
            pltpu.VMEM((seqs * SLOT_ROWS, 2 * inner), BF),
        ],
        compiler_params=params(22),
        cost_estimate=cost(us),
        name="attn_back",
    )(*streamed(gmb, xn, sel.reshape(seqs * SLOT_ROWS, width)), wo, *streamed(*kept), *after)


def input_back_kernel(
    x_ref, gm_ref, gain_ref, hot_ref, wqo, wqt, wko, wkt, wvo, wvt,
    dqo, dqt, dko, dkt, dvo, dvt, *refs,
):
    wq, wk, wv = refs[-3:]
    gx_ref, gp_ref, gg_ref = marked(refs[:-3])[-3:]
    first = pl.program_id(0) == 0
    inner = wqo.shape[1]
    length = x_ref.shape[0]

    @pl.when(first)
    def _():
        for cat, own, oth in ((wq, wqo, wqt), (wk, wko, wkt), (wv, wvo, wvt)):
            cat[:, :inner] = own[...]
            cat[:, inner:] = oth[...]

    dkeys = mm(jnp.concatenate([dko[0], dkt[0]], axis=1), wk[...], NT)
    dkeys += mm(jnp.concatenate([dvo[0], dvt[0]], axis=1), wv[...], NT)
    dxn = dkeys[:length] + mm(jnp.concatenate([dqo[...], dqt[...]], axis=1), wq[...], NT)
    x = x_ref[...].astype(F32)
    factor = lax.rsqrt(jnp.mean(x * x, axis=-1, keepdims=True) + EPS)
    scaled = x * factor
    c = gain_ref[...].reshape(1, -1) * dxn
    inner_mean = jnp.mean(c * scaled, axis=-1, keepdims=True)
    gx_ref[...] = gm_ref[...] + factor * (c - scaled * inner_mean)
    total = jnp.sum(dxn * scaled, axis=0, keepdims=True)
    gg_ref[...] = jnp.where(first, 0.0, gg_ref[...]) + total
    gp_ref[0] = mm(hot_ref[0], dkeys[length:].astype(BF))


def input_back(tokens, gm, gain_attn, hot, own, oth, d_own, d_oth, after=()):
    rows, width = tokens.shape
    seqs, keys, inner = d_own[1].shape
    length = rows // seqs
    pool_rows = hot.shape[1]
    row, head, key = rows_of(length, width), rows_of(length, inner), seq_of(keys, inner)
    return pl.pallas_call(
        input_back_kernel,
        grid=(seqs,),
        out_shape=[
            stored((rows, width), F32),
            sds((seqs, pool_rows, width), F32),
            sds((1, width), F32),
            MARK,
        ],
        in_specs=[
            row, row, whole((width,)), seq_of(pool_rows, SLOT_ROWS),
            *[whole((width, inner))] * 6, head, head, key, key, key, key, *[ANYWHERE] * len(after),
        ],
        out_specs=[row, seq_of(pool_rows, width), whole((1, width)), MARK_SPEC],
        scratch_shapes=[pltpu.VMEM((width, 2 * inner), BF)] * 3,
        compiler_params=params(22),
        cost_estimate=cost(8),
        name="input_back",
    )(
        *streamed(tokens, gm, gain_attn), *streamed(hot),
        *[w for pair in zip(streamed(*own[:3]), oth[:3]) for w in pair],
        *streamed(d_own[0], d_oth[0], d_own[1], d_oth[1], d_own[2], d_oth[2]), *after,
    )


def bf_sum(a, b):
    return (a.astype(F32) + b.astype(F32)).astype(BF)


def grid_steps(rows):
    return next((n for n in (4, 2) if rows % (16 * n) == 0 and rows // n >= 96), 1)


def halve_kernel(level, sides_ref, a_ref, b_ref, *refs):
    keep_ref, send_ref = marked(refs)[-2:]
    low, high = bf_sum(a_ref[0], b_ref[0]), bf_sum(a_ref[1], b_ref[1])
    upper = sides_ref[level] == 1
    keep_ref[...] = jnp.where(upper, high, low)
    send_ref[...] = jnp.where(upper, low, high)


def halve(level, sides, a, b, after=()):
    rows, width = a.shape[0] // 2, a.shape[1]
    steps = grid_steps(rows)
    pair = pl.BlockSpec((2, rows // steps, width), lambda j: (0, j, 0))
    half = rows_of(rows // steps, width)
    return pl.pallas_call(
        functools.partial(halve_kernel, level),
        grid=(steps,),
        out_shape=[sds((rows, width), BF)] * 2 + [MARK],
        in_specs=[IN_SMEM, pair, pair, *[ANYWHERE] * len(after)],
        out_specs=[half, half, MARK_SPEC],
        compiler_params=params(6),
        cost_estimate=cost(0.05),
        name="halve",
    )(sides, a.reshape(2, rows, width), b.reshape(2, rows, width), *after)


def add_kernel(a_ref, b_ref, *refs):
    marked(refs)[-1][...] = (a_ref[...].astype(F32) + b_ref[...].astype(F32)).astype(a_ref.dtype)


def add(a, b, after=()):
    full = whole(a.shape)
    return pl.pallas_call(
        add_kernel,
        out_shape=[sds(a.shape, a.dtype), MARK],
        in_specs=[full, full, *[ANYWHERE] * len(after)],
        out_specs=[full, MARK_SPEC],
        compiler_params=params(2),
        cost_estimate=cost(0.05),
        name="add",
    )(a, b, *after)


def joined(level, sides_ref, mine, got):
    upper = sides_ref[level] == 1
    return jnp.where(upper, got, mine), jnp.where(upper, mine, got)


def join_kernel(level, sides_ref, mine_ref, got_ref, *refs):
    out_ref = marked(refs)[-1]
    out_ref[0], out_ref[1] = joined(level, sides_ref, mine_ref[...], got_ref[...])


def join(level, sides, mine, got, after=()):
    rows, width = mine.shape
    steps = grid_steps(rows)
    part = rows_of(rows // steps, width)
    both, mark = pl.pallas_call(
        functools.partial(join_kernel, level),
        grid=(steps,),
        out_shape=[sds((2, rows, width), BF), MARK],
        in_specs=[IN_SMEM, part, part, *[ANYWHERE] * len(after)],
        out_specs=[pl.BlockSpec((2, rows // steps, width), lambda j: (0, j, 0)), MARK_SPEC],
        compiler_params=params(6),
        cost_estimate=cost(0.05),
        name="join",
    )(sides, mine, got, *after)
    return both.reshape(2 * rows, width), mark


def pool_join_kernel(mine_ref, got_ref, *refs):
    out_ref = marked(refs)[-1]
    first = lax.axis_index("mp") == 0
    mine, got = mine_ref[...], got_ref[...]
    seqs = mine.shape[0]
    out_ref[:seqs] = jnp.where(first, mine, got)
    out_ref[seqs:] = jnp.where(first, got, mine)


def pool_join(mine, got, after=()):
    full, shape = whole(mine.shape), (2 * mine.shape[0], *mine.shape[1:])
    return pl.pallas_call(
        pool_join_kernel,
        out_shape=[stored(shape, F32), MARK],
        in_specs=[full, full, *[ANYWHERE] * len(after)],
        out_specs=[whole(shape), MARK_SPEC],
        compiler_params=params(6),
        cost_estimate=cost(1),
        name="pool_join",
    )(mine, got, *after)


def ffn_finish_kernel(sides_ref, mine_ref, got_ref, *refs):
    down_ref, up_ref = marked(refs)[-2:]
    down, up = joined(0, sides_ref, mine_ref[...], got_ref[...])
    down_ref[...] = down.astype(F32)
    up_ref[...] = up.astype(F32)


def ffn_finish(index, count, sides, mine, got, before=(), after=()):
    width = mine.shape[1]
    steps = 4
    part = rows_of(width // steps, width)
    shapes = [stored((count * width, width), F32), stored((width, count * width), F32)]
    return pl.pallas_call(
        ffn_finish_kernel,
        grid=(steps,),
        out_shape=[*shapes, MARK],
        in_specs=[IN_SMEM, part, part, *[ANYWHERE] * (len(before) + len(after))],
        out_specs=[
            pl.BlockSpec((width // steps, width), lambda j: (index * steps + j, 0)),
            pl.BlockSpec((width // steps, width), lambda j: (j, index)),
            MARK_SPEC,
        ],
        input_output_aliases={3 + at: at for at in range(len(before))},
        compiler_params=params(10),
        cost_estimate=cost(2),
        name="ffn_finish",
    )(sides, mine, got, *before, *after)


def attn_finish_kernel(sides_ref, mine_ref, got_ref, *refs):
    wq_ref, wk_ref, wv_ref, wo_ref = refs[-4:]
    inner = wo_ref.shape[0]
    low, high = joined(0, sides_ref, mine_ref[...], got_ref[...])
    wo_ref[...] = low[:inner].astype(F32)
    for ref, stacked in ((wq_ref, low[inner:]), (wk_ref, high[:inner]), (wv_ref, high[inner:])):
        ref[:inner] = stacked[:, :inner].astype(F32)
        ref[inner:] = stacked[:, inner:].astype(F32)


def attn_finish(sides, mine, got, after=()):
    rows, width = mine.shape
    inner = rows // 2
    full = whole(mine.shape)
    return pl.pallas_call(
        attn_finish_kernel,
        out_shape=[stored((width, inner), F32)] * 3 + [stored((inner, width), F32)],
        in_specs=[IN_SMEM, full, full, *[ANYWHERE] * len(after)],
        out_specs=[whole((width, inner))] * 3 + [whole((inner, width))],
        compiler_params=params(14),
        cost_estimate=cost(2),
        name="attn_finish",
    )(sides, mine, got, *after)


class ChipSum:
    def __init__(self, dp, mp):
        bits = dp.bit_length() - 1
        here = lax.axis_index("dp")
        bit = [(here >> b) & 1 for b in range(bits)]
        if bits == 4:
            orders = ([1, 2, 4, 12], [2, 1, 12, 4])
            sides = (
                [bit[0], bit[1], bit[2] ^ bit[3], bit[3]],
                [bit[1], bit[0], bit[3], bit[2]],
            )
        else:
            swap = list(range(bits))
            swap[:2] = swap[:2][::-1]
            orders = ([1 << b for b in range(bits)], [1 << b for b in swap])
            sides = (bit, [bit[b] for b in swap])
        second = lax.axis_index("mp") % 2 == 1
        self.sides = jnp.where(second, jnp.stack(sides[1]), jnp.stack(sides[0]))
        self.levels = bits
        self.pairs = [
            [
                (d * mp + m, (d ^ orders[m % 2][b]) * mp + m)
                for d in range(dp)
                for m in range(mp)
            ]
            for b in range(bits)
        ]

    def exchange(self, level, array):
        return lax.ppermute(array, ("dp", "mp"), self.pairs[level])


class Group:
    def __init__(self, chips, mine, got, at=0):
        self.chips, self.mine, self.got, self.at = chips, mine, got, at

    @property
    def done(self):
        return self.at == 2 * self.chips.levels

    def step(self, after=()):
        chips, levels = self.chips, self.chips.levels
        level = self.at if self.at < levels else 2 * levels - 1 - self.at
        if self.at < levels:
            self.mine, sent, mark = halve(level, chips.sides, self.mine, self.got, after)
        elif self.at == levels:
            self.mine, mark = add(self.mine, self.got, after)
            sent = self.mine
        else:
            self.mine, mark = join(level + 1, chips.sides, self.mine, self.got, after)
            sent = self.mine
        self.got = chips.exchange(level, sent)
        self.at += 1
        return [mark]


class Small:
    def __init__(self, chips, array, got):
        self.chips, self.mine, self.got, self.at = chips, array, got, -1

    @property
    def done(self):
        return self.at == self.chips.levels

    def step(self, after=()):
        self.mine, mark = add(self.mine, self.got, after)
        self.at += 1
        if not self.done:
            self.got = self.chips.exchange(self.at, self.mine)
        return [mark]


def body(
    dp, mp, tokens, cotangent, w_query, key_projection_weight, value_projection_weight, w_out,
    w_up, w_down, gain_attn, gain_ffn, value_pool, slot_index, slot_count, pad_mask,
):
    seqs = tokens.shape[0] // pad_mask.shape[1]
    mine = (lax.axis_index("mp") * seqs)[None]

    def core_swap(array):
        return lax.ppermute(array, "mp", [(i, i ^ 1) for i in range(mp)])

    own = (w_query, key_projection_weight, value_projection_weight, w_out)
    oth = tuple(core_swap(w) for w in own)
    wu_oth, wd_oth = core_swap(w_up), core_swap(w_down)
    xn, sel, hot, first, second, middle, nf = attention_forward(
        tokens, gain_attn, gain_ffn, value_pool, slot_index, slot_count, pad_mask, seqs, mine,
        own, oth,
    )
    chips = ChipSum(dp, mp)
    count = w_up.shape[1] // w_up.shape[0]
    weights_oth, weights_own = (wu_oth, wd_oth), streamed(w_up, w_down)
    acts, dis, swapped, ffn, mark = [], [], [], [], []
    for at in range(count):
        act, di, grad, mark = ffn_part(at, nf, cotangent, weights_oth, (), mark)
        acts.append([act])
        dis.append([di])
        swapped.append(core_swap(grad))
        mark = [mark]
    for at in range(count):
        act, di, keep, send, mark = ffn_part(
            at, nf, cotangent, weights_own, (swapped[at], chips.sides), mark
        )
        acts[at].append(act)
        dis[at].append(di)
        ffn.append(Group(chips, keep, chips.exchange(0, send), 1))
        mark = [mark]
    acts, dis = sum(acts, []), sum(dis, [])
    gm, gmb, gg_ffn, mark = norm_back(cotangent, middle, gain_ffn, wu_oth, w_up, dis, mark)
    mark = ffn[0].step([mark])
    *d_oth, a_oth, mark = attn_back(gmb, xn, sel, oth[3], second, 1, mark)
    a_got = core_swap(a_oth)
    mark = ffn[0].step(ffn[1].step([mark]))
    *d_own, a_own, mark = attn_back(gmb, xn, sel, *streamed(w_out), first, 30, mark)
    attn = Group(chips, a_own, a_got)
    mark = ffn[1].step(ffn[0].step(attn.step([mark])))
    grad_tokens, grad_pool, gg_attn, mark = input_back(
        tokens, gm, gain_attn, hot, own, oth, d_own, d_oth, mark
    )
    pool_got = core_swap(grad_pool)
    gains = jnp.concatenate([gg_attn, gg_ffn], axis=0)
    gains = Small(chips, gains, core_swap(gains))
    mark = ffn[1].step(ffn[0].step(attn.step([mark])))
    block_out, mark = block_output(middle, wd_oth, w_down, acts, mark)
    grad_value_pool, mark = pool_join(grad_pool, pool_got, [mark])
    mark = [mark]
    ready = []
    while not attn.done or len(ready) < count or not gains.done:
        for at in range(count):
            if not ffn[at].done:
                mark = ffn[at].step(mark)
            elif len(ready) == at:
                out = ffn_finish(at, count, chips.sides, ffn[at].mine, ffn[at].got, ready[-1] if ready else (), mark)
                ready.append(out[:2])
                mark = [out[2]]
        if not attn.done:
            mark = attn.step(mark)
        if not gains.done:
            mark = gains.step(mark)
    grad_wd, grad_wu = ready[-1]
    grad_wq, grad_wk, grad_wv, grad_wo = attn_finish(chips.sides, attn.mine, attn.got, mark)
    return (
        block_out, grad_tokens, grad_wq, grad_wk, grad_wv, grad_wo, grad_wu, grad_wd,
        gains.mine[0], gains.mine[1], grad_value_pool,
    )


def solution(mesh):
    placed = (
        P(("dp", "mp"), None),
        P(("dp", "mp"), None),
        P(None, "mp"),
        P(None, "mp"),
        P(None, "mp"),
        P("mp", None),
        P(None, "mp"),
        P("mp", None),
        P(),
        P(),
        P("dp", None, None),
        P("dp", None),
        P("dp"),
        P("dp", None),
    )
    return jax.shard_map(
        functools.partial(body, mesh.shape["dp"], mesh.shape["mp"]),
        mesh=mesh,
        in_specs=placed,
        out_specs=(
            P(("dp", "mp"), None),
            P(("dp", "mp"), None),
            P(None, "mp"),
            P(None, "mp"),
            P(None, "mp"),
            P("mp", None),
            P(None, "mp"),
            P("mp", None),
            P(),
            P(),
            P("dp", None, None),
        ),
        check_vma=False,
    )
```

```python
import functools

import jax
import jax.numpy as jnp
from jax import lax
from jax.experimental import pallas as pl
from jax.experimental.pallas import tpu as pltpu
from jax.sharding import PartitionSpec as P

HDIM = 64
SCALE = HDIM ** (-0.5)
EPS = 1e-06
SLOT_ROWS = 32
BF = jnp.bfloat16
F32 = jnp.float32
MIB = 1 << 20

NN = (((1,), (0,)), ((), ()))
NT = (((1,), (1,)), ((), ()))
TN = (((0,), (0,)), ((), ()))
ANYWHERE = pl.BlockSpec(memory_space=pl.ANY)
IN_SMEM = pl.BlockSpec(memory_space=pltpu.SMEM)
sds = jax.ShapeDtypeStruct


def mm(left, right, dims=NN):
    return lax.dot_general(left, right, dims, preferred_element_type=F32)


def params(mib):
    return pltpu.CompilerParams(vmem_limit_bytes=mib * MIB)


def cost(us):
    return pl.CostEstimate(flops=int(us * 1.15e9), bytes_accessed=0, transcendentals=0)


def stored(shape, dtype):
    return pltpu.HBM(shape, dtype)


def streamed(*arrays):
    return [pltpu.with_memory_space_constraint(a, pltpu.HBM) for a in arrays]


def whole(shape):
    zeros = (0,) * len(shape)
    return pl.BlockSpec(shape, lambda *_: zeros)


def rows_of(rows, width):
    return pl.BlockSpec((rows, width), lambda s, *_: (s, 0))


def seq_of(*shape):
    tail = (0,) * len(shape)
    return pl.BlockSpec((1, *shape), lambda s, *_: (s, *tail))


MARK = sds((8, 128), F32)
MARK_SPEC = whole((8, 128))


def marked(refs):
    refs[-1][...] = jnp.zeros_like(refs[-1])
    return refs[:-1]


def head_masks():
    lanes = lax.broadcasted_iota(jnp.int32, (1, 2 * HDIM), 1)
    return lanes < HDIM, lanes >= HDIM


def pair_columns(width):
    return [slice(at, at + 2 * HDIM) for at in range(0, width, 2 * HDIM)]


def attend(q, k, v, bias, probs_ref):
    masks = head_masks()
    pieces = []
    for pair, cols in enumerate(pair_columns(q.shape[1])):
        qp, kp, vp = q[:, cols], k[:, cols], v[:, cols]
        mixed = None
        for half, mask in enumerate(masks):
            scores = mm(kp, jnp.where(mask, qp, 0), NT) + bias
            peak = jnp.max(scores, axis=0, keepdims=True)
            raised = jnp.exp(scores - peak)
            total = jnp.sum(raised, axis=0, keepdims=True)
            probs = (raised * (1.0 / total)).astype(BF)
            probs_ref[0, 2 * pair + half] = probs
            part = mm(probs, jnp.where(mask, vp, 0), TN)
            mixed = part if mixed is None else mixed + part
        pieces.append(mixed.astype(BF))
    return jnp.concatenate(pieces, axis=1)


def project(xn, sel, wq, wk, wv):
    rows = jnp.concatenate([xn, sel], axis=0)
    q = (mm(xn, wq) * SCALE).astype(BF)
    k = mm(rows, wk).astype(BF)
    v = mm(rows, wv).astype(BF)
    return q, k, v


def key_bias(seq, counts_ref, pads_ref, length):
    tokens = jnp.sum(pads_ref[pl.ds(seq, 1), :], axis=1, keepdims=True)
    token_ids = lax.broadcasted_iota(jnp.int32, (length, 1), 0)
    slot_ids = lax.broadcasted_iota(jnp.int32, (SLOT_ROWS, 1), 0)
    live = jnp.concatenate([token_ids < tokens, slot_ids < counts_ref[seq]], axis=0)
    return jnp.where(live, 0.0, -1e9).astype(F32)


def attn_first_kernel(
    first_ref, counts_ref, idx_ref, x_ref, gain_ref, pool_ref, pads_ref, wq_ref, wk_ref, wv_ref,
    xn_ref, sel_ref, bias_ref, hot_ref, q_ref, k_ref, v_ref, probs_ref, mixed_ref,
):
    seq = first_ref[0] + pl.program_id(0)
    x = x_ref[...].astype(F32)
    factor = lax.rsqrt(jnp.mean(x * x, axis=-1, keepdims=True) + EPS)
    xn = (x * factor * gain_ref[...].reshape(1, -1)).astype(BF)
    xn_ref[...] = xn
    spots = (pool_ref.shape[1], SLOT_ROWS)
    pool_ids = lax.broadcasted_iota(jnp.int32, spots, 0)
    slot_ids = lax.broadcasted_iota(jnp.int32, spots, 1)
    chosen = jnp.full(spots, -1, jnp.int32)
    for slot in range(idx_ref.shape[1]):
        chosen = jnp.where(slot_ids == slot, idx_ref[seq, slot], chosen)
    hot = jnp.where(chosen == pool_ids, 1.0, 0.0).astype(BF)
    hot_ref[0] = hot
    sel = mm(hot, pool_ref[0], TN).astype(BF)
    sel_ref[0] = sel
    bias = key_bias(seq, counts_ref, pads_ref, x_ref.shape[0])
    bias_ref[0] = bias
    q, k, v = project(xn, sel, wq_ref[...], wk_ref[...], wv_ref[...])
    q_ref[...] = q
    k_ref[0] = k
    v_ref[0] = v
    mixed_ref[...] = attend(q, k, v, bias, probs_ref)


def attn_second_kernel(
    x_ref, gain_ref, xn_ref, sel_ref, bias_ref, first_ref, wq_ref, wk_ref, wv_ref, woo_ref, wot_ref,
    q_ref, k_ref, v_ref, probs_ref, mixed_ref, middle_ref, nf_ref,
):
    q, k, v = project(xn_ref[...], sel_ref[0], wq_ref[...], wk_ref[...], wv_ref[...])
    q_ref[...] = q
    k_ref[0] = k
    v_ref[0] = v
    mixed = attend(q, k, v, bias_ref[0], probs_ref)
    mixed_ref[...] = mixed
    middle = x_ref[...].astype(F32) + mm(first_ref[...], woo_ref[...]) + mm(mixed, wot_ref[...])
    middle_ref[...] = middle
    factor = lax.rsqrt(jnp.mean(middle * middle, axis=-1, keepdims=True) + EPS)
    nf_ref[...] = (middle * factor * gain_ref[...].reshape(1, -1)).astype(BF)


def attention_forward(tokens, gain_attn, gain_ffn, pool, idx, counts, pads, seqs, mine, own, other):
    rows, width = tokens.shape
    length = rows // seqs
    keys = length + SLOT_ROWS
    inner = own[0].shape[1]
    heads = inner // HDIM
    row, head, key = rows_of(length, width), rows_of(length, inner), seq_of(keys, inner)
    kept = [
        (stored((rows, inner), BF), head),
        (stored((seqs, keys, inner), BF), key),
        (stored((seqs, keys, inner), BF), key),
        (stored((seqs, heads, keys, length), BF), seq_of(heads, keys, length)),
        (stored((rows, inner), BF), head),
    ]
    weight = whole((width, inner))
    outs = [
        (stored((rows, width), BF), row),
        (stored((seqs, SLOT_ROWS, width), BF), seq_of(SLOT_ROWS, width)),
        (stored((seqs, keys, 1), F32), seq_of(keys, 1)),
        (stored((seqs, pool.shape[1], SLOT_ROWS), BF), seq_of(pool.shape[1], SLOT_ROWS)),
        *kept,
    ]
    xn, sel, bias, hot, *first = pl.pallas_call(
        attn_first_kernel,
        grid_spec=pltpu.PrefetchScalarGridSpec(
            num_scalar_prefetch=3,
            grid=(seqs,),
            in_specs=[
                row,
                whole((width,)),
                pl.BlockSpec((1, *pool.shape[1:]), lambda s, first, *_: (first[0] + s, 0, 0)),
                whole(pads.shape),
                weight, weight, weight,
            ],
            out_specs=[o[1] for o in outs],
        ),
        out_shape=[o[0] for o in outs],
        compiler_params=params(14),
        cost_estimate=cost(12),
        name="attn_first",
    )(mine, counts, idx, *streamed(tokens, gain_attn, pool, pads, *own[:3]))
    outs = [
        *kept,
        (stored((rows, width), F32), row),
        (stored((rows, width), BF), row),
    ]
    *second, middle, nf = pl.pallas_call(
        attn_second_kernel,
        grid=(seqs,),
        out_shape=[o[0] for o in outs],
        in_specs=[
            row,
            whole((width,)),
            row,
            seq_of(SLOT_ROWS, width),
            seq_of(keys, 1),
            head,
            weight, weight, weight,
            whole((inner, width)),
            whole((inner, width)),
        ],
        out_specs=[o[1] for o in outs],
        compiler_params=params(18),
        cost_estimate=cost(12),
        name="attn_second",
    )(
        *streamed(tokens, gain_ffn),
        *streamed(xn, sel, bias, first[4]),
        *other[:3], *streamed(own[3]), other[3],
    )
    return xn, sel, hot, first, second, middle, nf


def gate_and_slope(h):
    c = 0.7978845608028654
    square = h * h
    t = jnp.tanh(h * (c + (c * 0.044715) * square))
    half = 0.5 + 0.5 * t
    slope = half + (0.5 * h) * (1.0 - t * t) * (c + (3.0 * c * 0.044715) * square)
    return h * half, slope


def ffn_kernel(own, chunk, nf_ref, cot_ref, wu_ref, wd_ref, *refs):
    rows = nf_ref.shape[0]
    units = wu_ref.shape[1]
    if own:
        got_ref, sides_ref = refs[:2]
        act_ref, di_ref, keep_ref, send_ref = marked(refs)[-4:]
    else:
        act_ref, di_ref, grad_ref = marked(refs)[-3:]
    wu, wd = wu_ref[...], wd_ref[...]
    for r in range(rows // chunk):
        at = slice(r * chunk, (r + 1) * chunk)
        act, slope = gate_and_slope(mm(nf_ref[at], wu))
        act_ref[at] = act.astype(BF)
        di_ref[at] = (mm(cot_ref[at], wd, NT) * slope).astype(BF)
    at = pl.ds(pl.multiple_of(pl.program_id(0) * units, units), units)
    down = mm(act_ref[...], cot_ref[...], TN).astype(BF)
    up = mm(nf_ref[...], di_ref[...], TN).astype(BF)
    if not own:
        grad_ref[0, at] = down
        grad_ref[1, :, at] = up
        return
    down = bf_sum(down, got_ref[0, at])
    up = bf_sum(up, got_ref[1, :, at])
    upper = sides_ref[0] == 1

    @pl.when(upper)
    def _():
        keep_ref[:, at] = up
        send_ref[at] = down

    @pl.when(jnp.logical_not(upper))
    def _():
        keep_ref[at] = down
        send_ref[:, at] = up


def ffn_part(index, nf, cot, weights, sums=(), after=()):
    rows, width = nf.shape
    own = len(sums) > 0
    units = 256
    steps = width // units
    full, square, part = whole((rows, width)), (width, width), pl.BlockSpec((rows, units), lambda j: (0, j))
    grads = [sds(square, BF)] * 2 if own else [sds((2, *square), BF)]
    extra = [whole((2, *square)), IN_SMEM] if own else []
    return pl.pallas_call(
        functools.partial(ffn_kernel, own, 256),
        grid=(steps,),
        out_shape=[*[stored((rows, width), BF)] * 2, *grads, MARK],
        in_specs=[
            full,
            full,
            pl.BlockSpec((width, units), lambda j: (0, index * steps + j)),
            pl.BlockSpec((units, width), lambda j: (index * steps + j, 0)),
            *extra,
            *[ANYWHERE] * len(after),
        ],
        out_specs=[part, part, *[whole(g.shape) for g in grads], MARK_SPEC],
        compiler_params=params(26),
        cost_estimate=cost(10),
        name="ffn_part",
    )(*streamed(nf, cot), *weights, *sums, *after)


def norm_back_kernel(cot_ref, middle_ref, gain_ref, wut_ref, wuo_ref, d0t, d0o, d1t, d1o, *refs):
    gm_ref, gmb_ref, gg_ref = marked(refs)[-3:]
    middle = middle_ref[...]
    width = middle.shape[1]
    dnf = 0.0
    for at, parts in enumerate(((d0t, d0o), (d1t, d1o))):
        cols = slice(at * width, (at + 1) * width)
        for part, wu_ref in zip(parts, (wut_ref, wuo_ref)):
            dnf += mm(part[...], wu_ref[:, cols], NT)
    factor = lax.rsqrt(jnp.mean(middle * middle, axis=-1, keepdims=True) + EPS)
    scaled = middle * factor
    e = gain_ref[...].reshape(1, -1) * dnf
    inner_mean = jnp.mean(e * scaled, axis=-1, keepdims=True)
    gm = cot_ref[...].astype(F32) + factor * (e - scaled * inner_mean)
    gm_ref[...] = gm
    gmb_ref[...] = gm.astype(BF)
    total = jnp.sum(dnf * scaled, axis=0, keepdims=True)
    gg_ref[...] = jnp.where(pl.program_id(0) == 0, 0.0, gg_ref[...]) + total


def norm_back(cot, middle, gain_ffn, wu_oth, wu_own, dis, after=()):
    rows, width = cot.shape
    block = 256
    row = rows_of(block, width)
    return pl.pallas_call(
        norm_back_kernel,
        grid=(rows // block,),
        out_shape=[stored((rows, width), F32), stored((rows, width), BF), sds((1, width), F32), MARK],
        in_specs=[
            row, row, whole((width,)), whole(wu_own.shape), whole(wu_own.shape), row, row, row, row,
            *[ANYWHERE] * len(after),
        ],
        out_specs=[row, row, whole((1, width)), MARK_SPEC],
        compiler_params=params(22),
        cost_estimate=cost(0.1),
        name="norm_back",
    )(*streamed(cot, middle, gain_ffn), wu_oth, *streamed(wu_own, *dis), *after)


def block_out_kernel(middle_ref, wdt_ref, wdo_ref, a0t, a0o, a1t, a1o, *refs):
    total = middle_ref[...]
    width = total.shape[1]
    for at, parts in enumerate(((a0t, a0o), (a1t, a1o))):
        for part, wd_ref in zip(parts, (wdt_ref, wdo_ref)):
            total += mm(part[...], wd_ref[at * width : (at + 1) * width])
    marked(refs)[-1][...] = total.astype(BF)


def block_output(middle, wd_oth, wd_own, acts, after=()):
    rows, width = middle.shape
    block = 256
    row = rows_of(block, width)
    return pl.pallas_call(
        block_out_kernel,
        grid=(rows // block,),
        out_shape=[stored((rows, width), BF), MARK],
        in_specs=[
            row, whole(wd_own.shape), whole(wd_own.shape), row, row, row, row, *[ANYWHERE] * len(after),
        ],
        out_specs=[row, MARK_SPEC],
        compiler_params=params(18),
        cost_estimate=cost(0.1),
        name="block_out",
    )(*streamed(middle), wd_oth, *streamed(wd_own, *acts), *after)


def stack(grad):
    part = grad.shape[1]
    return jnp.concatenate([grad[at : at + part] for at in range(0, grad.shape[0], part)], axis=1)


def unstack_to(ref, at, stacked):
    part = stacked.shape[0]
    for block in range(stacked.shape[1] // part):
        rows = slice(block * part, (block + 1) * part)
        ref[rows, at : at + part] = stacked[:, rows].astype(F32)


def attn_back_kernel(
    gm_ref, xn_ref, selall_ref, wo_ref, q_ref, k_ref, v_ref, p_ref, m_ref, *refs
):
    awo, aw, slots = refs[-3:]
    dq_ref, dk_ref, dv_ref, grad_ref = marked(refs[:-3])[-4:]
    step = pl.program_id(0)
    masks = head_masks()
    gm, xn = gm_ref[...], xn_ref[...]
    length = gm.shape[0]

    @pl.when(step == 0)
    def _():
        awo[...] = jnp.zeros_like(awo)
        aw[...] = jnp.zeros_like(aw)

    awo[...] += mm(m_ref[...], gm, TN)
    dmix = mm(gm, wo_ref[...], NT).astype(BF)
    dqs, dks, dvs = [], [], []
    for pair, cols in enumerate(pair_columns(dmix.shape[1])):
        qp, kp, vp, dp = q_ref[:, cols], k_ref[0, :, cols], v_ref[0, :, cols], dmix[:, cols]
        dq = dk = dv = 0.0
        for half, mask in enumerate(masks):
            probs = p_ref[0, 2 * pair + half]
            dp_head = jnp.where(mask, dp, 0)
            weighted = mm(vp, dp_head, NT)
            high = probs.astype(F32)
            delta = jnp.sum(high * weighted, axis=0, keepdims=True)
            ds = (high * (weighted - delta)).astype(BF)
            dv += mm(probs, dp_head)
            dq += mm(ds, jnp.where(mask, kp, 0), TN)
            dk += mm(ds, jnp.where(mask, qp, 0))
        dqs.append((dq * SCALE).astype(BF))
        dks.append(dk.astype(BF))
        dvs.append(dv.astype(BF))
    dq, dk, dv = [jnp.concatenate(d, axis=1) for d in (dqs, dks, dvs)]
    dq_ref[...] = dq
    dk_ref[0] = dk
    dv_ref[0] = dv
    aw[...] += mm(xn, jnp.concatenate([dq, dk[:length], dv[:length]], axis=1), TN)
    at = pl.ds(pl.multiple_of(step * SLOT_ROWS, SLOT_ROWS), SLOT_ROWS)
    slots[at] = jnp.concatenate([dk[length:], dv[length:]], axis=1)

    @pl.when(step == pl.num_programs(0) - 1)
    def _():
        inner = awo.shape[0]
        grad_ref[:inner] = awo[...].astype(BF)
        grad_ref[inner : 2 * inner] = stack(aw[:, :inner].astype(BF))
        rest = (aw[:, inner:] + mm(selall_ref[...], slots[...], TN)).astype(BF)
        grad_ref[2 * inner : 3 * inner] = stack(rest[:, :inner])
        grad_ref[3 * inner :] = stack(rest[:, inner:])


def attn_back(gmb, xn, sel, wo, kept, at, inner, us, after=()):
    rows, width = gmb.shape
    seqs, _, keys, length = kept[3].shape
    heads = inner // HDIM
    block = at // inner
    row = rows_of(length, width)
    head_in = pl.BlockSpec((length, inner), lambda s: (s, block))
    key_in = pl.BlockSpec((1, keys, inner), lambda s: (s, 0, block))
    grads = sds((4 * inner, width), BF)
    outs = [
        (stored((rows, inner), BF), rows_of(length, inner)),
        (stored((seqs, keys, inner), BF), seq_of(keys, inner)),
        (stored((seqs, keys, inner), BF), seq_of(keys, inner)),
        (grads, whole(grads.shape)),
        (MARK, MARK_SPEC),
    ]
    return pl.pallas_call(
        attn_back_kernel,
        grid=(seqs,),
        out_shape=[o[0] for o in outs],
        in_specs=[
            row, row, whole((seqs * SLOT_ROWS, width)),
            pl.BlockSpec((inner, width), lambda s: (block, 0)),
            head_in, key_in, key_in,
            pl.BlockSpec((1, heads, keys, length), lambda s: (s, block, 0, 0)),
            head_in, *[ANYWHERE] * len(after),
        ],
        out_specs=[o[1] for o in outs],
        scratch_shapes=[
            pltpu.VMEM((inner, width), F32),
            pltpu.VMEM((width, 3 * inner), F32),
            pltpu.VMEM((seqs * SLOT_ROWS, 2 * inner), BF),
        ],
        compiler_params=params(22),
        cost_estimate=cost(us),
        name="attn_back",
    )(*streamed(gmb, xn, sel.reshape(seqs * SLOT_ROWS, width)), wo, *streamed(*kept), *after)


def input_back_kernel(
    parts, x_ref, gm_ref, gain_ref, hot_ref, wqo, wqt, wko, wkt, wvo, wvt,
    *refs,
):
    grads, refs = refs[: 3 * parts], refs[3 * parts :]
    dq = jnp.concatenate([g[...] for g in grads[:parts]], axis=1)
    dk = jnp.concatenate([g[0] for g in grads[parts : 2 * parts]], axis=1)
    dv = jnp.concatenate([g[0] for g in grads[2 * parts :]], axis=1)
    wq, wk, wv = refs[-3:]
    gx_ref, gp_ref, gg_ref = marked(refs[:-3])[-3:]
    first = pl.program_id(0) == 0
    inner = wqo.shape[1]
    length = x_ref.shape[0]

    @pl.when(first)
    def _():
        for cat, own, oth in ((wq, wqo, wqt), (wk, wko, wkt), (wv, wvo, wvt)):
            cat[:, :inner] = own[...]
            cat[:, inner:] = oth[...]

    dkeys = mm(dk, wk[...], NT) + mm(dv, wv[...], NT)
    dxn = dkeys[:length] + mm(dq, wq[...], NT)
    x = x_ref[...].astype(F32)
    factor = lax.rsqrt(jnp.mean(x * x, axis=-1, keepdims=True) + EPS)
    scaled = x * factor
    c = gain_ref[...].reshape(1, -1) * dxn
    inner_mean = jnp.mean(c * scaled, axis=-1, keepdims=True)
    gx_ref[...] = gm_ref[...] + factor * (c - scaled * inner_mean)
    total = jnp.sum(dxn * scaled, axis=0, keepdims=True)
    gg_ref[...] = jnp.where(first, 0.0, gg_ref[...]) + total
    gp_ref[0] = mm(hot_ref[0], dkeys[length:].astype(BF))


def input_back(tokens, gm, gain_attn, hot, own, oth, grads, after=()):
    rows, width = tokens.shape
    seqs, keys = grads[0][1].shape[:2]
    length = rows // seqs
    pool_rows, inner = hot.shape[1], own[0].shape[1]
    row = rows_of(length, width)
    flat = [g[kind] for kind in range(3) for g in grads]
    return pl.pallas_call(
        functools.partial(input_back_kernel, len(grads)),
        grid=(seqs,),
        out_shape=[
            stored((rows, width), F32),
            sds((seqs, pool_rows, width), F32),
            sds((1, width), F32),
            MARK,
        ],
        in_specs=[
            row, row, whole((width,)), seq_of(pool_rows, SLOT_ROWS),
            *[whole((width, inner))] * 6,
            *[rows_of(length, g[0].shape[1]) for g in grads],
            *[seq_of(keys, g[0].shape[1]) for g in [*grads, *grads]],
            *[ANYWHERE] * len(after),
        ],
        out_specs=[row, seq_of(pool_rows, width), whole((1, width)), MARK_SPEC],
        scratch_shapes=[pltpu.VMEM((width, 2 * inner), BF)] * 3,
        compiler_params=params(22),
        cost_estimate=cost(0.1),
        name="input_back",
    )(
        *streamed(tokens, gm, gain_attn, hot),
        *[w for pair in zip(streamed(*own[:3]), oth[:3]) for w in pair],
        *streamed(*flat), *after,
    )


def bf_sum(a, b):
    return (a.astype(F32) + b.astype(F32)).astype(BF)


def grid_steps(rows):
    return next((n for n in (4, 2) if rows % (16 * n) == 0 and rows // n >= 96), 1)


def halve_kernel(level, sides_ref, a_ref, b_ref, *refs):
    keep_ref, send_ref = marked(refs)[-2:]
    low, high = bf_sum(a_ref[0], b_ref[0]), bf_sum(a_ref[1], b_ref[1])
    upper = sides_ref[level] == 1
    keep_ref[...] = jnp.where(upper, high, low)
    send_ref[...] = jnp.where(upper, low, high)


def halve(level, sides, a, b, after=()):
    rows, width = a.shape[0] // 2, a.shape[1]
    steps = grid_steps(rows)
    pair = pl.BlockSpec((2, rows // steps, width), lambda j: (0, j, 0))
    half = rows_of(rows // steps, width)
    return pl.pallas_call(
        functools.partial(halve_kernel, level),
        grid=(steps,),
        out_shape=[sds((rows, width), BF)] * 2 + [MARK],
        in_specs=[IN_SMEM, pair, pair, *[ANYWHERE] * len(after)],
        out_specs=[half, half, MARK_SPEC],
        compiler_params=params(6),
        cost_estimate=cost(0.05),
        name="halve",
    )(sides, a.reshape(2, rows, width), b.reshape(2, rows, width), *after)


def open_kernel(sides_ref, *refs):
    keep_ref, send_ref = marked(refs)[-2:]
    upper = sides_ref[0] == 1
    at = 0
    for own_ref, got_ref in zip(refs[::2], refs[1::2]):
        if len(own_ref.shape) != 3 or at == keep_ref.shape[0]:
            break
        rows = own_ref.shape[1]
        low, high = bf_sum(own_ref[0], got_ref[0]), bf_sum(own_ref[1], got_ref[1])
        keep_ref[at : at + rows] = jnp.where(upper, high, low)
        send_ref[at : at + rows] = jnp.where(upper, low, high)
        at += rows


def open_sums(sides, owns, gots, after=()):
    width = owns[0].shape[1]
    arrays = [a.reshape(2, -1, width) for pair in zip(owns, gots) for a in pair]
    rows = sum(o.shape[0] for o in owns) // 2
    return pl.pallas_call(
        open_kernel,
        out_shape=[sds((rows, width), BF)] * 2 + [MARK],
        in_specs=[IN_SMEM, *[whole(a.shape) for a in arrays], *[ANYWHERE] * len(after)],
        out_specs=[whole((rows, width))] * 2 + [MARK_SPEC],
        compiler_params=params(14),
        cost_estimate=cost(0.05),
        name="open_sums",
    )(sides, *arrays, *after)


def add_kernel(a_ref, b_ref, *refs):
    marked(refs)[-1][...] = (a_ref[...].astype(F32) + b_ref[...].astype(F32)).astype(a_ref.dtype)


def add(a, b, after=()):
    full = whole(a.shape)
    return pl.pallas_call(
        add_kernel,
        out_shape=[sds(a.shape, a.dtype), MARK],
        in_specs=[full, full, *[ANYWHERE] * len(after)],
        out_specs=[full, MARK_SPEC],
        compiler_params=params(2),
        cost_estimate=cost(0.05),
        name="add",
    )(a, b, *after)


def joined(level, sides_ref, mine, got):
    upper = sides_ref[level] == 1
    return jnp.where(upper, got, mine), jnp.where(upper, mine, got)


def join_kernel(level, sides_ref, mine_ref, got_ref, *refs):
    out_ref = marked(refs)[-1]
    out_ref[0], out_ref[1] = joined(level, sides_ref, mine_ref[...], got_ref[...])


def join(level, sides, mine, got, after=()):
    rows, width = mine.shape
    steps = grid_steps(rows)
    part = rows_of(rows // steps, width)
    both, mark = pl.pallas_call(
        functools.partial(join_kernel, level),
        grid=(steps,),
        out_shape=[sds((2, rows, width), BF), MARK],
        in_specs=[IN_SMEM, part, part, *[ANYWHERE] * len(after)],
        out_specs=[pl.BlockSpec((2, rows // steps, width), lambda j: (0, j, 0)), MARK_SPEC],
        compiler_params=params(6),
        cost_estimate=cost(0.05),
        name="join",
    )(sides, mine, got, *after)
    return both.reshape(2 * rows, width), mark


def pool_join_kernel(mine_ref, got_ref, *refs):
    out_ref = marked(refs)[-1]
    first = lax.axis_index("mp") == 0
    mine, got = mine_ref[...], got_ref[...]
    seqs = mine.shape[0]
    out_ref[:seqs] = jnp.where(first, mine, got)
    out_ref[seqs:] = jnp.where(first, got, mine)


def pool_join(mine, got, after=()):
    full, shape = whole(mine.shape), (2 * mine.shape[0], *mine.shape[1:])
    return pl.pallas_call(
        pool_join_kernel,
        out_shape=[stored(shape, F32), MARK],
        in_specs=[full, full, *[ANYWHERE] * len(after)],
        out_specs=[whole(shape), MARK_SPEC],
        compiler_params=params(6),
        cost_estimate=cost(1),
        name="pool_join",
    )(mine, got, *after)


def ffn_finish_kernel(sides_ref, mine_ref, got_ref, *refs):
    down_ref, up_ref = marked(refs)[-2:]
    down, up = joined(0, sides_ref, mine_ref[...], got_ref[...])
    down_ref[...] = down.astype(F32)
    up_ref[...] = up.astype(F32)


def ffn_finish(index, count, sides, mine, got, before=(), after=()):
    width = mine.shape[1]
    steps = 4
    part = rows_of(width // steps, width)
    shapes = [stored((count * width, width), F32), stored((width, count * width), F32)]
    return pl.pallas_call(
        ffn_finish_kernel,
        grid=(steps,),
        out_shape=[*shapes, MARK],
        in_specs=[IN_SMEM, part, part, *[ANYWHERE] * (len(before) + len(after))],
        out_specs=[
            pl.BlockSpec((width // steps, width), lambda j: (index * steps + j, 0)),
            pl.BlockSpec((width // steps, width), lambda j: (j, index)),
            MARK_SPEC,
        ],
        input_output_aliases={3 + at: at for at in range(len(before))},
        compiler_params=params(10),
        cost_estimate=cost(0.05),
        name="ffn_finish",
    )(sides, mine, got, *before, *after)


def attn_finish_kernel(parts, sides_ref, mine_ref, got_ref, *refs):
    wq_ref, wk_ref, wv_ref, wo_ref = refs[-4:]
    low, high = joined(0, sides_ref, mine_ref[...], got_ref[...])
    at = column = 0
    for part in parts:
        wo_ref[column : column + part] = low[at : at + part].astype(F32)
        unstack_to(wq_ref, column, low[at + part : at + 2 * part])
        unstack_to(wk_ref, column, high[at : at + part])
        unstack_to(wv_ref, column, high[at + part : at + 2 * part])
        at, column = at + 2 * part, column + part


def attn_finish(parts, sides, mine, got, after=()):
    rows, width = mine.shape
    inner = rows // 2
    full = whole(mine.shape)
    return pl.pallas_call(
        functools.partial(attn_finish_kernel, parts),
        out_shape=[stored((width, inner), F32)] * 3 + [stored((inner, width), F32)],
        in_specs=[IN_SMEM, full, full, *[ANYWHERE] * len(after)],
        out_specs=[whole((width, inner))] * 3 + [whole((inner, width))],
        compiler_params=params(14),
        cost_estimate=cost(2),
        name="attn_finish",
    )(sides, mine, got, *after)


class ChipSum:
    def __init__(self, dp, mp):
        bits = dp.bit_length() - 1
        here = lax.axis_index("dp")
        bit = [(here >> b) & 1 for b in range(bits)]
        if bits == 4:
            orders = ([1, 2, 4, 12], [2, 1, 12, 4])
            sides = (
                [bit[0], bit[1], bit[2] ^ bit[3], bit[3]],
                [bit[1], bit[0], bit[3], bit[2]],
            )
        else:
            swap = list(range(bits))
            swap[:2] = swap[:2][::-1]
            orders = ([1 << b for b in range(bits)], [1 << b for b in swap])
            sides = (bit, [bit[b] for b in swap])
        second = lax.axis_index("mp") % 2 == 1
        self.sides = jnp.where(second, jnp.stack(sides[1]), jnp.stack(sides[0]))
        self.levels = bits
        self.pairs = [
            [
                (d * mp + m, (d ^ orders[m % 2][b]) * mp + m)
                for d in range(dp)
                for m in range(mp)
            ]
            for b in range(bits)
        ]

    def exchange(self, level, array):
        return lax.ppermute(array, ("dp", "mp"), self.pairs[level])


class Group:
    def __init__(self, chips, mine, got, at=0):
        self.chips, self.mine, self.got, self.at = chips, mine, got, at

    @property
    def done(self):
        return self.at == 2 * self.chips.levels

    def step(self, after=()):
        chips, levels = self.chips, self.chips.levels
        level = self.at if self.at < levels else 2 * levels - 1 - self.at
        if self.at < levels:
            self.mine, sent, mark = halve(level, chips.sides, self.mine, self.got, after)
        elif self.at == levels:
            self.mine, mark = add(self.mine, self.got, after)
            sent = self.mine
        else:
            self.mine, mark = join(level + 1, chips.sides, self.mine, self.got, after)
            sent = self.mine
        self.got = chips.exchange(level, sent)
        self.at += 1
        return [mark]


class Small:
    def __init__(self, chips, array, got):
        self.chips, self.mine, self.got, self.at = chips, array, got, -1

    @property
    def done(self):
        return self.at == self.chips.levels

    def step(self, after=()):
        self.mine, mark = add(self.mine, self.got, after)
        self.at += 1
        if not self.done:
            self.got = self.chips.exchange(self.at, self.mine)
        return [mark]


def arrived(groups):
    return [g.got for g in groups]


def body(
    dp, mp, tokens, cotangent, w_query, key_projection_weight, value_projection_weight, w_out,
    w_up, w_down, gain_attn, gain_ffn, value_pool, slot_index, slot_count, pad_mask,
):
    seqs = tokens.shape[0] // pad_mask.shape[1]
    mine = (lax.axis_index("mp") * seqs)[None]

    def core_swap(array):
        return lax.ppermute(array, "mp", [(i, i ^ 1) for i in range(mp)])

    own = (w_query, key_projection_weight, value_projection_weight, w_out)
    oth = tuple(core_swap(w) for w in own)
    wu_oth, wd_oth = core_swap(w_up), core_swap(w_down)
    xn, sel, hot, first, second, middle, nf = attention_forward(
        tokens, gain_attn, gain_ffn, value_pool, slot_index, slot_count, pad_mask, seqs, mine,
        own, oth,
    )
    chips = ChipSum(dp, mp)
    count = w_up.shape[1] // w_up.shape[0]
    weights_oth, weights_own = (wu_oth, wd_oth), streamed(w_up, w_down)
    acts, dis, swapped, ffn, mark = [], [], [], [], []
    for at in range(count):
        act, di, grad, mark = ffn_part(at, nf, cotangent, weights_oth, (), mark)
        acts.append([act])
        dis.append([di])
        swapped.append(core_swap(grad))
        mark = [mark]
    for at in range(count):
        act, di, keep, send, mark = ffn_part(
            at, nf, cotangent, weights_own, (swapped[at], chips.sides), mark
        )
        acts[at].append(act)
        dis[at].append(di)
        ffn.append(Group(chips, keep, chips.exchange(0, send), 1))
        mark = [mark]
    acts, dis = sum(acts, []), sum(dis, [])
    gm, gmb, gg_ffn, mark = norm_back(cotangent, middle, gain_ffn, wu_oth, w_up, dis, mark)
    mark = ffn[0].step([mark])
    parts, starts = (256, 128), (0, 256)
    assert sum(parts) == w_out.shape[0]
    d_own, d_oth, a_own, a_got = [], [], [], []
    for at, part in zip(starts, parts):
        *d, grad, mark = attn_back(gmb, xn, sel, oth[3], second, at, part, 0.1, mark)
        d_oth.append(d)
        a_got.append(core_swap(grad))
        mark = ffn[1].step(ffn[0].step([mark, *arrived(ffn)]))
    for at, part in zip(starts, parts):
        *d, grad, mark = attn_back(
            gmb, xn, sel, *streamed(w_out), first, at, part, 22, mark
        )
        d_own.append(d)
        a_own.append(grad)
        if len(a_own) < len(parts):
            mark = ffn[1].step(ffn[0].step([mark, *arrived(ffn)]))
    keep, send, mark = open_sums(chips.sides, a_own, a_got, [mark, *arrived(ffn)])
    attn = Group(chips, keep, chips.exchange(0, send), 1)
    mark = ffn[1].step(ffn[0].step([mark]))
    grad_tokens, grad_pool, gg_attn, mark = input_back(
        tokens, gm, gain_attn, hot, own, oth, [*d_own, *d_oth], mark
    )
    pool_got = core_swap(grad_pool)
    gains = jnp.concatenate([gg_attn, gg_ffn], axis=0)
    gains = Small(chips, gains, core_swap(gains))
    mark = gains.step(ffn[1].step(ffn[0].step(attn.step([mark, *arrived(ffn)]))))
    block_out, mark = block_output(middle, wd_oth, w_down, acts, mark)
    grad_value_pool, mark = pool_join(grad_pool, pool_got, [mark])
    mark = [mark]
    last = 2 * chips.levels
    ready = []
    late = [0] * count
    while attn.at < last or not gains.done:
        waited = [g for g, l in zip(ffn, late) if g.at < last or l == 1]
        late = [l + (g.at == last) for g, l in zip(ffn, late)]
        if attn.at < last:
            mark = attn.step([*mark, *arrived([*waited, *([] if gains.done else [gains])])])
        for group in ffn:
            if group.at < last:
                mark = group.step(mark)
        if not gains.done:
            mark = gains.step(mark)
    while len(ready) < count:
        at = len(ready)
        *out, mark = ffn_finish(
            at, count, chips.sides, ffn[at].mine, ffn[at].got, ready[-1] if ready else (), mark
        )
        ready.append(out)
        mark = [mark]
    grad_wd, grad_wu = ready[-1]
    grad_wq, grad_wk, grad_wv, grad_wo = attn_finish(parts, chips.sides, attn.mine, attn.got, mark)
    return (
        block_out, grad_tokens, grad_wq, grad_wk, grad_wv, grad_wo, grad_wu, grad_wd,
        gains.mine[0], gains.mine[1], grad_value_pool,
    )


def solution(mesh):
    placed = (
        P(("dp", "mp"), None),
        P(("dp", "mp"), None),
        P(None, "mp"),
        P(None, "mp"),
        P(None, "mp"),
        P("mp", None),
        P(None, "mp"),
        P("mp", None),
        P(),
        P(),
        P("dp", None, None),
        P("dp", None),
        P("dp"),
        P("dp", None),
    )
    return jax.shard_map(
        functools.partial(body, mesh.shape["dp"], mesh.shape["mp"]),
        mesh=mesh,
        in_specs=placed,
        out_specs=(
            P(("dp", "mp"), None),
            P(("dp", "mp"), None),
            P(None, "mp"),
            P(None, "mp"),
            P(None, "mp"),
            P("mp", None),
            P(None, "mp"),
            P("mp", None),
            P(),
            P(),
            P("dp", None, None),
        ),
        check_vma=False,
    )
```

```python
import functools

import jax
import jax.numpy as jnp
from jax import lax
from jax.experimental import pallas as pl
from jax.experimental.pallas import tpu as pltpu
from jax.sharding import PartitionSpec as P

HDIM = 64
SCALE = HDIM ** (-0.5)
EPS = 1e-06
SLOT_ROWS = 32
BF = jnp.bfloat16
F32 = jnp.float32
MIB = 1 << 20

NN = (((1,), (0,)), ((), ()))
NT = (((1,), (1,)), ((), ()))
TN = (((0,), (0,)), ((), ()))
ANYWHERE = pl.BlockSpec(memory_space=pl.ANY)
IN_SMEM = pl.BlockSpec(memory_space=pltpu.SMEM)
sds = jax.ShapeDtypeStruct


def mm(left, right, dims=NN):
    return lax.dot_general(left, right, dims, preferred_element_type=F32)


def params(mib):
    return pltpu.CompilerParams(vmem_limit_bytes=mib * MIB)


def cost(us):
    return pl.CostEstimate(flops=int(us * 1.15e9), bytes_accessed=0, transcendentals=0)


def stored(shape, dtype):
    return pltpu.HBM(shape, dtype)


def streamed(*arrays):
    return [pltpu.with_memory_space_constraint(a, pltpu.HBM) for a in arrays]


def whole(shape):
    zeros = (0,) * len(shape)
    return pl.BlockSpec(shape, lambda *_: zeros)


def rows_of(rows, width):
    return pl.BlockSpec((rows, width), lambda s, *_: (s, 0))


def seq_of(*shape):
    tail = (0,) * len(shape)
    return pl.BlockSpec((1, *shape), lambda s, *_: (s, *tail))


MARK = sds((8, 128), F32)
MARK_SPEC = whole((8, 128))


def marked(refs):
    refs[-1][...] = jnp.zeros_like(refs[-1])
    return refs[:-1]


def head_masks():
    lanes = lax.broadcasted_iota(jnp.int32, (1, 2 * HDIM), 1)
    return lanes < HDIM, lanes >= HDIM


def pair_columns(width):
    return [slice(at, at + 2 * HDIM) for at in range(0, width, 2 * HDIM)]


def attend(q, k, v, bias, probs_ref):
    masks = head_masks()
    pieces = []
    for pair, cols in enumerate(pair_columns(q.shape[1])):
        qp, kp, vp = q[:, cols], k[:, cols], v[:, cols]
        mixed = None
        for half, mask in enumerate(masks):
            scores = mm(kp, jnp.where(mask, qp, 0), NT) + bias
            peak = jnp.max(scores, axis=0, keepdims=True)
            raised = jnp.exp(scores - peak)
            total = jnp.sum(raised, axis=0, keepdims=True)
            probs = (raised * (1.0 / total)).astype(BF)
            probs_ref[0, 2 * pair + half] = probs
            part = mm(probs, jnp.where(mask, vp, 0), TN)
            mixed = part if mixed is None else mixed + part
        pieces.append(mixed.astype(BF))
    return jnp.concatenate(pieces, axis=1)


def project(xn, sel, wq, wk, wv):
    rows = jnp.concatenate([xn, sel], axis=0)
    q = (mm(xn, wq) * SCALE).astype(BF)
    k = mm(rows, wk).astype(BF)
    v = mm(rows, wv).astype(BF)
    return q, k, v


def key_bias(seq, counts_ref, pads_ref, length):
    tokens = jnp.sum(pads_ref[pl.ds(seq, 1), :], axis=1, keepdims=True)
    token_ids = lax.broadcasted_iota(jnp.int32, (length, 1), 0)
    slot_ids = lax.broadcasted_iota(jnp.int32, (SLOT_ROWS, 1), 0)
    live = jnp.concatenate([token_ids < tokens, slot_ids < counts_ref[seq]], axis=0)
    return jnp.where(live, 0.0, -1e9).astype(F32)


def attn_first_kernel(
    first_ref, counts_ref, idx_ref, x_ref, gain_ref, pool_ref, pads_ref, wq_ref, wk_ref, wv_ref,
    xn_ref, sel_ref, bias_ref, hot_ref, q_ref, k_ref, v_ref, probs_ref, mixed_ref,
):
    seq = first_ref[0] + pl.program_id(0)
    x = x_ref[...].astype(F32)
    factor = lax.rsqrt(jnp.mean(x * x, axis=-1, keepdims=True) + EPS)
    xn = (x * factor * gain_ref[...].reshape(1, -1)).astype(BF)
    xn_ref[...] = xn
    spots = (pool_ref.shape[1], SLOT_ROWS)
    pool_ids = lax.broadcasted_iota(jnp.int32, spots, 0)
    slot_ids = lax.broadcasted_iota(jnp.int32, spots, 1)
    chosen = jnp.full(spots, -1, jnp.int32)
    for slot in range(idx_ref.shape[1]):
        chosen = jnp.where(slot_ids == slot, idx_ref[seq, slot], chosen)
    hot = jnp.where(chosen == pool_ids, 1.0, 0.0).astype(BF)
    hot_ref[0] = hot
    sel = mm(hot, pool_ref[0], TN).astype(BF)
    sel_ref[0] = sel
    bias = key_bias(seq, counts_ref, pads_ref, x_ref.shape[0])
    bias_ref[0] = bias
    q, k, v = project(xn, sel, wq_ref[...], wk_ref[...], wv_ref[...])
    q_ref[...] = q
    k_ref[0] = k
    v_ref[0] = v
    mixed_ref[...] = attend(q, k, v, bias, probs_ref)


def attn_second_kernel(
    x_ref, gain_ref, xn_ref, sel_ref, bias_ref, first_ref, wq_ref, wk_ref, wv_ref, woo_ref, wot_ref,
    q_ref, k_ref, v_ref, probs_ref, mixed_ref, middle_ref, nf_ref,
):
    q, k, v = project(xn_ref[...], sel_ref[0], wq_ref[...], wk_ref[...], wv_ref[...])
    q_ref[...] = q
    k_ref[0] = k
    v_ref[0] = v
    mixed = attend(q, k, v, bias_ref[0], probs_ref)
    mixed_ref[...] = mixed
    middle = x_ref[...].astype(F32) + mm(first_ref[...], woo_ref[...]) + mm(mixed, wot_ref[...])
    middle_ref[...] = middle
    factor = lax.rsqrt(jnp.mean(middle * middle, axis=-1, keepdims=True) + EPS)
    nf_ref[...] = (middle * factor * gain_ref[...].reshape(1, -1)).astype(BF)


def attention_forward(tokens, gain_attn, gain_ffn, pool, idx, counts, pads, seqs, mine, own, other):
    rows, width = tokens.shape
    length = rows // seqs
    keys = length + SLOT_ROWS
    inner = own[0].shape[1]
    heads = inner // HDIM
    row, head, key = rows_of(length, width), rows_of(length, inner), seq_of(keys, inner)
    kept = [
        (stored((rows, inner), BF), head),
        (stored((seqs, keys, inner), BF), key),
        (stored((seqs, keys, inner), BF), key),
        (stored((seqs, heads, keys, length), BF), seq_of(heads, keys, length)),
        (stored((rows, inner), BF), head),
    ]
    weight = whole((width, inner))
    outs = [
        (stored((rows, width), BF), row),
        (stored((seqs, SLOT_ROWS, width), BF), seq_of(SLOT_ROWS, width)),
        (stored((seqs, keys, 1), F32), seq_of(keys, 1)),
        (stored((seqs, pool.shape[1], SLOT_ROWS), BF), seq_of(pool.shape[1], SLOT_ROWS)),
        *kept,
    ]
    xn, sel, bias, hot, *first = pl.pallas_call(
        attn_first_kernel,
        grid_spec=pltpu.PrefetchScalarGridSpec(
            num_scalar_prefetch=3,
            grid=(seqs,),
            in_specs=[
                row,
                whole((width,)),
                pl.BlockSpec((1, *pool.shape[1:]), lambda s, first, *_: (first[0] + s, 0, 0)),
                whole(pads.shape),
                weight, weight, weight,
            ],
            out_specs=[o[1] for o in outs],
        ),
        out_shape=[o[0] for o in outs],
        compiler_params=params(14),
        cost_estimate=cost(12),
        name="attn_first",
    )(mine, counts, idx, *streamed(tokens, gain_attn, pool, pads, *own[:3]))
    outs = [
        *kept,
        (stored((rows, width), F32), row),
        (stored((rows, width), BF), row),
    ]
    *second, middle, nf = pl.pallas_call(
        attn_second_kernel,
        grid=(seqs,),
        out_shape=[o[0] for o in outs],
        in_specs=[
            row,
            whole((width,)),
            row,
            seq_of(SLOT_ROWS, width),
            seq_of(keys, 1),
            head,
            weight, weight, weight,
            whole((inner, width)),
            whole((inner, width)),
        ],
        out_specs=[o[1] for o in outs],
        compiler_params=params(18),
        cost_estimate=cost(12),
        name="attn_second",
    )(
        *streamed(tokens, gain_ffn),
        *streamed(xn, sel, bias, first[4]),
        *other[:3], *streamed(own[3]), other[3],
    )
    return xn, sel, hot, first, second, middle, nf


def gate_and_slope(h):
    c = 0.7978845608028654
    square = h * h
    t = jnp.tanh(h * (c + (c * 0.044715) * square))
    half = 0.5 + 0.5 * t
    slope = half + (0.5 * h) * (1.0 - t * t) * (c + (3.0 * c * 0.044715) * square)
    return h * half, slope


def ffn_kernel(own, chunk, nf_ref, cot_ref, wu_ref, wd_ref, *refs):
    rows = nf_ref.shape[0]
    units = wu_ref.shape[1]
    if own:
        got_ref, sides_ref = refs[:2]
        act_ref, di_ref, keep_ref, send_ref = marked(refs)[-4:]
    else:
        act_ref, di_ref, grad_ref = marked(refs)[-3:]
    wu, wd = wu_ref[...], wd_ref[...]
    for r in range(rows // chunk):
        at = slice(r * chunk, (r + 1) * chunk)
        act, slope = gate_and_slope(mm(nf_ref[at], wu))
        act_ref[at] = act.astype(BF)
        di_ref[at] = (mm(cot_ref[at], wd, NT) * slope).astype(BF)
    at = pl.ds(pl.multiple_of(pl.program_id(0) * units, units), units)
    down = mm(act_ref[...], cot_ref[...], TN).astype(BF)
    up = mm(nf_ref[...], di_ref[...], TN).astype(BF)
    if not own:
        grad_ref[0, at] = down
        grad_ref[1, :, at] = up
        return
    down = bf_sum(down, got_ref[0, at])
    up = bf_sum(up, got_ref[1, :, at])
    upper = sides_ref[0] == 1

    @pl.when(upper)
    def _():
        keep_ref[:, at] = up
        send_ref[at] = down

    @pl.when(jnp.logical_not(upper))
    def _():
        keep_ref[at] = down
        send_ref[:, at] = up


def ffn_part(index, nf, cot, weights, sums=(), after=()):
    rows, width = nf.shape
    own = len(sums) > 0
    units = 256
    steps = width // units
    full, square, part = whole((rows, width)), (width, width), pl.BlockSpec((rows, units), lambda j: (0, j))
    grads = [sds(square, BF)] * 2 if own else [sds((2, *square), BF)]
    extra = [whole((2, *square)), IN_SMEM] if own else []
    return pl.pallas_call(
        functools.partial(ffn_kernel, own, 256),
        grid=(steps,),
        out_shape=[*[stored((rows, width), BF)] * 2, *grads, MARK],
        in_specs=[
            full,
            full,
            pl.BlockSpec((width, units), lambda j: (0, index * steps + j)),
            pl.BlockSpec((units, width), lambda j: (index * steps + j, 0)),
            *extra,
            *[ANYWHERE] * len(after),
        ],
        out_specs=[part, part, *[whole(g.shape) for g in grads], MARK_SPEC],
        compiler_params=params(26),
        cost_estimate=cost(10),
        name="ffn_part",
    )(*streamed(nf, cot), *weights, *sums, *after)


def norm_back_kernel(cot_ref, middle_ref, gain_ref, wut_ref, wuo_ref, d0t, d0o, d1t, d1o, *refs):
    gm_ref, gmb_ref, gg_ref = marked(refs)[-3:]
    middle = middle_ref[...]
    width = middle.shape[1]
    dnf = 0.0
    for at, parts in enumerate(((d0t, d0o), (d1t, d1o))):
        cols = slice(at * width, (at + 1) * width)
        for part, wu_ref in zip(parts, (wut_ref, wuo_ref)):
            dnf += mm(part[...], wu_ref[:, cols], NT)
    factor = lax.rsqrt(jnp.mean(middle * middle, axis=-1, keepdims=True) + EPS)
    scaled = middle * factor
    e = gain_ref[...].reshape(1, -1) * dnf
    inner_mean = jnp.mean(e * scaled, axis=-1, keepdims=True)
    gm = cot_ref[...].astype(F32) + factor * (e - scaled * inner_mean)
    gm_ref[...] = gm
    gmb_ref[...] = gm.astype(BF)
    total = jnp.sum(dnf * scaled, axis=0, keepdims=True)
    gg_ref[...] = jnp.where(pl.program_id(0) == 0, 0.0, gg_ref[...]) + total


def norm_back(cot, middle, gain_ffn, wu_oth, wu_own, dis, after=()):
    rows, width = cot.shape
    block = 256
    row = rows_of(block, width)
    return pl.pallas_call(
        norm_back_kernel,
        grid=(rows // block,),
        out_shape=[stored((rows, width), F32), stored((rows, width), BF), sds((1, width), F32), MARK],
        in_specs=[
            row, row, whole((width,)), whole(wu_own.shape), whole(wu_own.shape), row, row, row, row,
            *[ANYWHERE] * len(after),
        ],
        out_specs=[row, row, whole((1, width)), MARK_SPEC],
        compiler_params=params(22),
        cost_estimate=cost(0.1),
        name="norm_back",
    )(*streamed(cot, middle, gain_ffn), wu_oth, *streamed(wu_own, *dis), *after)


def block_out_kernel(middle_ref, wdt_ref, wdo_ref, a0t, a0o, a1t, a1o, *refs):
    total = middle_ref[...]
    width = total.shape[1]
    for at, parts in enumerate(((a0t, a0o), (a1t, a1o))):
        for part, wd_ref in zip(parts, (wdt_ref, wdo_ref)):
            total += mm(part[...], wd_ref[at * width : (at + 1) * width])
    marked(refs)[-1][...] = total.astype(BF)


def block_output(middle, wd_oth, wd_own, acts, after=()):
    rows, width = middle.shape
    block = 256
    row = rows_of(block, width)
    return pl.pallas_call(
        block_out_kernel,
        grid=(rows // block,),
        out_shape=[stored((rows, width), BF), MARK],
        in_specs=[
            row, whole(wd_own.shape), whole(wd_own.shape), row, row, row, row, *[ANYWHERE] * len(after),
        ],
        out_specs=[row, MARK_SPEC],
        compiler_params=params(18),
        cost_estimate=cost(0.1),
        name="block_out",
    )(*streamed(middle), wd_oth, *streamed(wd_own, *acts), *after)


def stack(grad):
    part = grad.shape[1]
    return jnp.concatenate([grad[at : at + part] for at in range(0, grad.shape[0], part)], axis=1)


def unstack_to(ref, at, stacked):
    part = stacked.shape[0]
    for block in range(stacked.shape[1] // part):
        rows = slice(block * part, (block + 1) * part)
        ref[rows, at : at + part] = stacked[:, rows].astype(F32)


def attn_back_kernel(
    gm_ref, xn_ref, selall_ref, wo_ref, q_ref, k_ref, v_ref, p_ref, m_ref, *refs
):
    awo, aw, slots = refs[-3:]
    dq_ref, dk_ref, dv_ref, grad_ref = marked(refs[:-3])[-4:]
    step = pl.program_id(0)
    masks = head_masks()
    gm, xn = gm_ref[...], xn_ref[...]
    length = gm.shape[0]

    @pl.when(step == 0)
    def _():
        awo[...] = jnp.zeros_like(awo)
        aw[...] = jnp.zeros_like(aw)

    awo[...] += mm(m_ref[...], gm, TN)
    dmix = mm(gm, wo_ref[...], NT).astype(BF)
    dqs, dks, dvs = [], [], []
    for pair, cols in enumerate(pair_columns(dmix.shape[1])):
        qp, kp, vp, dp = q_ref[:, cols], k_ref[0, :, cols], v_ref[0, :, cols], dmix[:, cols]
        dq = dk = dv = 0.0
        for half, mask in enumerate(masks):
            probs = p_ref[0, 2 * pair + half]
            dp_head = jnp.where(mask, dp, 0)
            weighted = mm(vp, dp_head, NT)
            high = probs.astype(F32)
            delta = jnp.sum(high * weighted, axis=0, keepdims=True)
            ds = (high * (weighted - delta)).astype(BF)
            dv += mm(probs, dp_head)
            dq += mm(ds, jnp.where(mask, kp, 0), TN)
            dk += mm(ds, jnp.where(mask, qp, 0))
        dqs.append((dq * SCALE).astype(BF))
        dks.append(dk.astype(BF))
        dvs.append(dv.astype(BF))
    dq, dk, dv = [jnp.concatenate(d, axis=1) for d in (dqs, dks, dvs)]
    dq_ref[...] = dq
    dk_ref[0] = dk
    dv_ref[0] = dv
    aw[...] += mm(xn, jnp.concatenate([dq, dk[:length], dv[:length]], axis=1), TN)
    at = pl.ds(pl.multiple_of(step * SLOT_ROWS, SLOT_ROWS), SLOT_ROWS)
    slots[at] = jnp.concatenate([dk[length:], dv[length:]], axis=1)

    @pl.when(step == pl.num_programs(0) - 1)
    def _():
        inner = awo.shape[0]
        grad_ref[:inner] = awo[...].astype(BF)
        grad_ref[inner : 2 * inner] = stack(aw[:, :inner].astype(BF))
        rest = (aw[:, inner:] + mm(selall_ref[...], slots[...], TN)).astype(BF)
        grad_ref[2 * inner : 3 * inner] = stack(rest[:, :inner])
        grad_ref[3 * inner :] = stack(rest[:, inner:])


def attn_back(gmb, xn, sel, wo, kept, at, inner, us, after=()):
    rows, width = gmb.shape
    seqs, _, keys, length = kept[3].shape
    heads = inner // HDIM
    block = at // inner
    row = rows_of(length, width)
    head_in = pl.BlockSpec((length, inner), lambda s: (s, block))
    key_in = pl.BlockSpec((1, keys, inner), lambda s: (s, 0, block))
    grads = sds((4 * inner, width), BF)
    outs = [
        (stored((rows, inner), BF), rows_of(length, inner)),
        (stored((seqs, keys, inner), BF), seq_of(keys, inner)),
        (stored((seqs, keys, inner), BF), seq_of(keys, inner)),
        (grads, whole(grads.shape)),
        (MARK, MARK_SPEC),
    ]
    return pl.pallas_call(
        attn_back_kernel,
        grid=(seqs,),
        out_shape=[o[0] for o in outs],
        in_specs=[
            row, row, whole((seqs * SLOT_ROWS, width)),
            pl.BlockSpec((inner, width), lambda s: (block, 0)),
            head_in, key_in, key_in,
            pl.BlockSpec((1, heads, keys, length), lambda s: (s, block, 0, 0)),
            head_in, *[ANYWHERE] * len(after),
        ],
        out_specs=[o[1] for o in outs],
        scratch_shapes=[
            pltpu.VMEM((inner, width), F32),
            pltpu.VMEM((width, 3 * inner), F32),
            pltpu.VMEM((seqs * SLOT_ROWS, 2 * inner), BF),
        ],
        compiler_params=params(22),
        cost_estimate=cost(us),
        name="attn_back",
    )(*streamed(gmb, xn, sel.reshape(seqs * SLOT_ROWS, width)), wo, *streamed(*kept), *after)


def input_back_kernel(
    parts, x_ref, gm_ref, gain_ref, hot_ref, wqo, wqt, wko, wkt, wvo, wvt,
    *refs,
):
    grads, refs = refs[: 3 * parts], refs[3 * parts :]
    dq = jnp.concatenate([g[...] for g in grads[:parts]], axis=1)
    dk = jnp.concatenate([g[0] for g in grads[parts : 2 * parts]], axis=1)
    dv = jnp.concatenate([g[0] for g in grads[2 * parts :]], axis=1)
    wq, wk, wv = refs[-3:]
    gx_ref, gp_ref, gg_ref = marked(refs[:-3])[-3:]
    first = pl.program_id(0) == 0
    inner = wqo.shape[1]
    length = x_ref.shape[0]

    @pl.when(first)
    def _():
        for cat, own, oth in ((wq, wqo, wqt), (wk, wko, wkt), (wv, wvo, wvt)):
            cat[:, :inner] = own[...]
            cat[:, inner:] = oth[...]

    dkeys = mm(dk, wk[...], NT) + mm(dv, wv[...], NT)
    dxn = dkeys[:length] + mm(dq, wq[...], NT)
    x = x_ref[...].astype(F32)
    factor = lax.rsqrt(jnp.mean(x * x, axis=-1, keepdims=True) + EPS)
    scaled = x * factor
    c = gain_ref[...].reshape(1, -1) * dxn
    inner_mean = jnp.mean(c * scaled, axis=-1, keepdims=True)
    gx_ref[...] = gm_ref[...] + factor * (c - scaled * inner_mean)
    total = jnp.sum(dxn * scaled, axis=0, keepdims=True)
    gg_ref[...] = jnp.where(first, 0.0, gg_ref[...]) + total
    gp_ref[0] = mm(hot_ref[0], dkeys[length:].astype(BF))


def input_back(tokens, gm, gain_attn, hot, own, oth, grads, after=()):
    rows, width = tokens.shape
    seqs, keys = grads[0][1].shape[:2]
    length = rows // seqs
    pool_rows, inner = hot.shape[1], own[0].shape[1]
    row = rows_of(length, width)
    flat = [g[kind] for kind in range(3) for g in grads]
    return pl.pallas_call(
        functools.partial(input_back_kernel, len(grads)),
        grid=(seqs,),
        out_shape=[
            stored((rows, width), F32),
            sds((seqs, pool_rows, width), F32),
            sds((1, width), F32),
            MARK,
        ],
        in_specs=[
            row, row, whole((width,)), seq_of(pool_rows, SLOT_ROWS),
            *[whole((width, inner))] * 6,
            *[rows_of(length, g[0].shape[1]) for g in grads],
            *[seq_of(keys, g[0].shape[1]) for g in [*grads, *grads]],
            *[ANYWHERE] * len(after),
        ],
        out_specs=[row, seq_of(pool_rows, width), whole((1, width)), MARK_SPEC],
        scratch_shapes=[pltpu.VMEM((width, 2 * inner), BF)] * 3,
        compiler_params=params(22),
        cost_estimate=cost(0.1),
        name="input_back",
    )(
        *streamed(tokens, gm, gain_attn, hot),
        *[w for pair in zip(streamed(*own[:3]), oth[:3]) for w in pair],
        *streamed(*flat), *after,
    )


def bf_sum(a, b):
    return (a.astype(F32) + b.astype(F32)).astype(BF)


def grid_steps(rows):
    return next((n for n in (4, 2) if rows % (16 * n) == 0 and rows // n >= 96), 1)


def halve_kernel(level, sides_ref, a_ref, b_ref, *refs):
    keep_ref, send_ref = marked(refs)[-2:]
    low, high = bf_sum(a_ref[0], b_ref[0]), bf_sum(a_ref[1], b_ref[1])
    upper = sides_ref[level] == 1
    keep_ref[...] = jnp.where(upper, high, low)
    send_ref[...] = jnp.where(upper, low, high)


def halve(level, sides, a, b, after=()):
    rows, width = a.shape[0] // 2, a.shape[1]
    steps = grid_steps(rows)
    pair = pl.BlockSpec((2, rows // steps, width), lambda j: (0, j, 0))
    half = rows_of(rows // steps, width)
    return pl.pallas_call(
        functools.partial(halve_kernel, level),
        grid=(steps,),
        out_shape=[sds((rows, width), BF)] * 2 + [MARK],
        in_specs=[IN_SMEM, pair, pair, *[ANYWHERE] * len(after)],
        out_specs=[half, half, MARK_SPEC],
        compiler_params=params(6),
        cost_estimate=cost(0.05),
        name="halve",
    )(sides, a.reshape(2, rows, width), b.reshape(2, rows, width), *after)


def open_kernel(sides_ref, *refs):
    keep_ref, send_ref = marked(refs)[-2:]
    upper = sides_ref[0] == 1
    at = 0
    for own_ref, got_ref in zip(refs[::2], refs[1::2]):
        if len(own_ref.shape) != 3 or at == keep_ref.shape[0]:
            break
        rows = own_ref.shape[1]
        low, high = bf_sum(own_ref[0], got_ref[0]), bf_sum(own_ref[1], got_ref[1])
        keep_ref[at : at + rows] = jnp.where(upper, high, low)
        send_ref[at : at + rows] = jnp.where(upper, low, high)
        at += rows


def open_sums(sides, owns, gots, after=()):
    width = owns[0].shape[1]
    arrays = [a.reshape(2, -1, width) for pair in zip(owns, gots) for a in pair]
    rows = sum(o.shape[0] for o in owns) // 2
    return pl.pallas_call(
        open_kernel,
        out_shape=[sds((rows, width), BF)] * 2 + [MARK],
        in_specs=[IN_SMEM, *[whole(a.shape) for a in arrays], *[ANYWHERE] * len(after)],
        out_specs=[whole((rows, width))] * 2 + [MARK_SPEC],
        compiler_params=params(14),
        cost_estimate=cost(0.05),
        name="open_sums",
    )(sides, *arrays, *after)


def add_kernel(a_ref, b_ref, *refs):
    marked(refs)[-1][...] = (a_ref[...].astype(F32) + b_ref[...].astype(F32)).astype(a_ref.dtype)


def add(a, b, after=()):
    full = whole(a.shape)
    return pl.pallas_call(
        add_kernel,
        out_shape=[sds(a.shape, a.dtype), MARK],
        in_specs=[full, full, *[ANYWHERE] * len(after)],
        out_specs=[full, MARK_SPEC],
        compiler_params=params(2),
        cost_estimate=cost(0.05),
        name="add",
    )(a, b, *after)


def joined(level, sides_ref, mine, got):
    upper = sides_ref[level] == 1
    return jnp.where(upper, got, mine), jnp.where(upper, mine, got)


def join_kernel(level, sides_ref, mine_ref, got_ref, *refs):
    out_ref = marked(refs)[-1]
    out_ref[0], out_ref[1] = joined(level, sides_ref, mine_ref[...], got_ref[...])


def join(level, sides, mine, got, after=()):
    rows, width = mine.shape
    steps = grid_steps(rows)
    part = rows_of(rows // steps, width)
    both, mark = pl.pallas_call(
        functools.partial(join_kernel, level),
        grid=(steps,),
        out_shape=[sds((2, rows, width), BF), MARK],
        in_specs=[IN_SMEM, part, part, *[ANYWHERE] * len(after)],
        out_specs=[pl.BlockSpec((2, rows // steps, width), lambda j: (0, j, 0)), MARK_SPEC],
        compiler_params=params(6),
        cost_estimate=cost(0.05),
        name="join",
    )(sides, mine, got, *after)
    return both.reshape(2 * rows, width), mark


def pool_join_kernel(mine_ref, got_ref, *refs):
    out_ref = marked(refs)[-1]
    first = lax.axis_index("mp") == 0
    mine, got = mine_ref[...], got_ref[...]
    seqs = mine.shape[0]
    out_ref[:seqs] = jnp.where(first, mine, got)
    out_ref[seqs:] = jnp.where(first, got, mine)


def pool_join(mine, got, after=()):
    full, shape = whole(mine.shape), (2 * mine.shape[0], *mine.shape[1:])
    return pl.pallas_call(
        pool_join_kernel,
        out_shape=[stored(shape, F32), MARK],
        in_specs=[full, full, *[ANYWHERE] * len(after)],
        out_specs=[whole(shape), MARK_SPEC],
        compiler_params=params(6),
        cost_estimate=cost(1),
        name="pool_join",
    )(mine, got, *after)


def ffn_finish_kernel(sides_ref, mine_ref, got_ref, *refs):
    down_ref, up_ref = marked(refs)[-2:]
    down, up = joined(0, sides_ref, mine_ref[...], got_ref[...])
    down_ref[...] = down.astype(F32)
    up_ref[...] = up.astype(F32)


def ffn_finish(index, count, sides, mine, got, before=(), after=()):
    width = mine.shape[1]
    steps = 4
    part = rows_of(width // steps, width)
    shapes = [stored((count * width, width), F32), stored((width, count * width), F32)]
    return pl.pallas_call(
        ffn_finish_kernel,
        grid=(steps,),
        out_shape=[*shapes, MARK],
        in_specs=[IN_SMEM, part, part, *[ANYWHERE] * (len(before) + len(after))],
        out_specs=[
            pl.BlockSpec((width // steps, width), lambda j: (index * steps + j, 0)),
            pl.BlockSpec((width // steps, width), lambda j: (j, index)),
            MARK_SPEC,
        ],
        input_output_aliases={3 + at: at for at in range(len(before))},
        compiler_params=params(10),
        cost_estimate=cost(0.05),
        name="ffn_finish",
    )(sides, mine, got, *before, *after)


def attn_finish_kernel(parts, sides_ref, mine_ref, got_ref, *refs):
    wq_ref, wk_ref, wv_ref, wo_ref = refs[-4:]
    low, high = joined(0, sides_ref, mine_ref[...], got_ref[...])
    at = column = 0
    for part in parts:
        wo_ref[column : column + part] = low[at : at + part].astype(F32)
        unstack_to(wq_ref, column, low[at + part : at + 2 * part])
        unstack_to(wk_ref, column, high[at : at + part])
        unstack_to(wv_ref, column, high[at + part : at + 2 * part])
        at, column = at + 2 * part, column + part


def attn_finish(parts, sides, mine, got, after=()):
    rows, width = mine.shape
    inner = rows // 2
    full = whole(mine.shape)
    return pl.pallas_call(
        functools.partial(attn_finish_kernel, parts),
        out_shape=[stored((width, inner), F32)] * 3 + [stored((inner, width), F32)],
        in_specs=[IN_SMEM, full, full, *[ANYWHERE] * len(after)],
        out_specs=[whole((width, inner))] * 3 + [whole((inner, width))],
        compiler_params=params(14),
        cost_estimate=cost(2),
        name="attn_finish",
    )(sides, mine, got, *after)


class ChipSum:
    def __init__(self, dp, mp):
        bits = dp.bit_length() - 1
        here = lax.axis_index("dp")
        bit = [(here >> b) & 1 for b in range(bits)]
        if bits == 4:
            orders = ([1, 2, 4, 12], [2, 1, 12, 4])
            sides = (
                [bit[0], bit[1], bit[2] ^ bit[3], bit[3]],
                [bit[1], bit[0], bit[3], bit[2]],
            )
        else:
            swap = list(range(bits))
            swap[:2] = swap[:2][::-1]
            orders = ([1 << b for b in range(bits)], [1 << b for b in swap])
            sides = (bit, [bit[b] for b in swap])
        second = lax.axis_index("mp") % 2 == 1
        self.sides = jnp.where(second, jnp.stack(sides[1]), jnp.stack(sides[0]))
        self.levels = bits
        self.pairs = [
            [
                (d * mp + m, (d ^ orders[m % 2][b]) * mp + m)
                for d in range(dp)
                for m in range(mp)
            ]
            for b in range(bits)
        ]

        masks = [1 << b for b in range(bits)]
        self.turns = [
            [(d * mp + m, (d ^ mask) * mp + m) for d in range(dp) for m in range(mp)]
            for mask in masks[:1] + masks[2:] + masks[1:2]
        ]

    def turn(self, at, array):
        return lax.ppermute(array, ("dp", "mp"), self.turns[at])

    def exchange(self, level, array):
        return lax.ppermute(array, ("dp", "mp"), self.pairs[level])


class Group:
    def __init__(self, chips, mine, got, at=0):
        self.chips, self.mine, self.got, self.at = chips, mine, got, at

    @property
    def done(self):
        return self.at == 2 * self.chips.levels

    def step(self, after=()):
        chips, levels = self.chips, self.chips.levels
        level = self.at if self.at < levels else 2 * levels - 1 - self.at
        if self.at < levels:
            self.mine, sent, mark = halve(level, chips.sides, self.mine, self.got, after)
        elif self.at == levels:
            self.mine, mark = add(self.mine, self.got, after)
            sent = self.mine
        else:
            self.mine, mark = join(level + 1, chips.sides, self.mine, self.got, after)
            sent = self.mine
        self.got = chips.exchange(level, sent)
        self.at += 1
        return [mark]


class Small:
    def __init__(self, chips, array, got):
        self.chips, self.mine, self.got, self.at = chips, array, got, -1

    @property
    def done(self):
        return self.at == self.chips.levels

    def step(self, after=()):
        self.mine, mark = add(self.mine, self.got, after)
        self.at += 1
        if not self.done:
            self.got = self.chips.turn(self.at, self.mine)
        return [mark]


def arrived(groups):
    return [g.got for g in groups]


def body(
    dp, mp, tokens, cotangent, w_query, key_projection_weight, value_projection_weight, w_out,
    w_up, w_down, gain_attn, gain_ffn, value_pool, slot_index, slot_count, pad_mask,
):
    seqs = tokens.shape[0] // pad_mask.shape[1]
    mine = (lax.axis_index("mp") * seqs)[None]

    def core_swap(array):
        return lax.ppermute(array, "mp", [(i, i ^ 1) for i in range(mp)])

    own = (w_query, key_projection_weight, value_projection_weight, w_out)
    oth = tuple(core_swap(w) for w in own)
    wu_oth, wd_oth = core_swap(w_up), core_swap(w_down)
    xn, sel, hot, first, second, middle, nf = attention_forward(
        tokens, gain_attn, gain_ffn, value_pool, slot_index, slot_count, pad_mask, seqs, mine,
        own, oth,
    )
    chips = ChipSum(dp, mp)
    count = w_up.shape[1] // w_up.shape[0]
    weights_oth, weights_own = (wu_oth, wd_oth), streamed(w_up, w_down)
    acts, dis, swapped, ffn, mark = [], [], [], [], []
    for at in range(count):
        act, di, grad, mark = ffn_part(at, nf, cotangent, weights_oth, (), mark)
        acts.append([act])
        dis.append([di])
        swapped.append(core_swap(grad))
        mark = [mark]
    for at in range(count):
        act, di, keep, send, mark = ffn_part(
            at, nf, cotangent, weights_own, (swapped[at], chips.sides), mark
        )
        acts[at].append(act)
        dis[at].append(di)
        ffn.append(Group(chips, keep, chips.exchange(0, send), 1))
        mark = [mark]
    acts, dis = sum(acts, []), sum(dis, [])
    gm, gmb, gg_ffn, mark = norm_back(cotangent, middle, gain_ffn, wu_oth, w_up, dis, mark)
    mark = ffn[0].step([mark])
    parts, starts = (256, 128), (0, 256)
    assert sum(parts) == w_out.shape[0]
    d_own, d_oth, a_own, a_got = [], [], [], []
    for at, part in zip(starts, parts):
        *d, grad, mark = attn_back(gmb, xn, sel, oth[3], second, at, part, 0.1, mark)
        d_oth.append(d)
        a_got.append(core_swap(grad))
        mark = ffn[1].step(ffn[0].step([mark, *arrived(ffn)]))
    for at, part in zip(starts, parts):
        *d, grad, mark = attn_back(
            gmb, xn, sel, *streamed(w_out), first, at, part, 22, mark
        )
        d_own.append(d)
        a_own.append(grad)
        if len(a_own) < len(parts):
            mark = ffn[1].step(ffn[0].step([mark, *arrived(ffn)]))
    keep, send, mark = open_sums(chips.sides, a_own, a_got, [mark, *arrived(ffn)])
    attn = Group(chips, keep, chips.exchange(0, send), 1)
    mark = ffn[1].step(ffn[0].step([mark]))
    grad_tokens, grad_pool, gg_attn, mark = input_back(
        tokens, gm, gain_attn, hot, own, oth, [*d_own, *d_oth], mark
    )
    pool_got = core_swap(grad_pool)
    gains = jnp.concatenate([gg_attn, gg_ffn], axis=0)
    gains = Small(chips, gains, core_swap(gains))
    mark = gains.step(ffn[1].step(ffn[0].step(attn.step([mark, *arrived(ffn)]))))
    block_out, mark = block_output(middle, wd_oth, w_down, acts, mark)
    grad_value_pool, mark = pool_join(grad_pool, pool_got, [mark])
    mark = [mark]
    last = 2 * chips.levels
    ready = []
    late = [0] * count
    while attn.at < last or not gains.done:
        waited = [g for g, l in zip(ffn, late) if g.at < last or l == 1]
        late = [l + (g.at == last) for g, l in zip(ffn, late)]
        if attn.at < last:
            mark = attn.step([*mark, *arrived([*waited, *([] if gains.done else [gains])])])
        for group in ffn:
            if group.at < last:
                mark = group.step(mark)
        if not gains.done:
            mark = gains.step(mark)
    while len(ready) < count:
        at = len(ready)
        *out, mark = ffn_finish(
            at, count, chips.sides, ffn[at].mine, ffn[at].got, ready[-1] if ready else (), mark
        )
        ready.append(out)
        mark = [mark]
    grad_wd, grad_wu = ready[-1]
    grad_wq, grad_wk, grad_wv, grad_wo = attn_finish(parts, chips.sides, attn.mine, attn.got, mark)
    return (
        block_out, grad_tokens, grad_wq, grad_wk, grad_wv, grad_wo, grad_wu, grad_wd,
        gains.mine[0], gains.mine[1], grad_value_pool,
    )


def solution(mesh):
    placed = (
        P(("dp", "mp"), None),
        P(("dp", "mp"), None),
        P(None, "mp"),
        P(None, "mp"),
        P(None, "mp"),
        P("mp", None),
        P(None, "mp"),
        P("mp", None),
        P(),
        P(),
        P("dp", None, None),
        P("dp", None),
        P("dp"),
        P("dp", None),
    )
    return jax.shard_map(
        functools.partial(body, mesh.shape["dp"], mesh.shape["mp"]),
        mesh=mesh,
        in_specs=placed,
        out_specs=(
            P(("dp", "mp"), None),
            P(("dp", "mp"), None),
            P(None, "mp"),
            P(None, "mp"),
            P(None, "mp"),
            P("mp", None),
            P(None, "mp"),
            P("mp", None),
            P(),
            P(),
            P("dp", None, None),
        ),
        check_vma=False,
    )
```

```python
import functools

import jax
import jax.numpy as jnp
from jax import lax
from jax.experimental import pallas as pl
from jax.experimental.pallas import tpu as pltpu
from jax.sharding import PartitionSpec as P

HDIM = 64
SCALE = HDIM ** (-0.5)
EPS = 1e-06
SLOT_ROWS = 32
BF = jnp.bfloat16
F32 = jnp.float32
MIB = 1 << 20

NN = (((1,), (0,)), ((), ()))
NT = (((1,), (1,)), ((), ()))
TN = (((0,), (0,)), ((), ()))
ANYWHERE = pl.BlockSpec(memory_space=pl.ANY)
IN_SMEM = pl.BlockSpec(memory_space=pltpu.SMEM)
sds = jax.ShapeDtypeStruct


def mm(left, right, dims=NN):
    return lax.dot_general(left, right, dims, preferred_element_type=F32)


def params(mib):
    return pltpu.CompilerParams(vmem_limit_bytes=mib * MIB)


def cost(us):
    return pl.CostEstimate(flops=int(us * 1.15e9), bytes_accessed=0, transcendentals=0)


def stored(shape, dtype):
    return pltpu.HBM(shape, dtype)


def streamed(*arrays):
    return [pltpu.with_memory_space_constraint(a, pltpu.HBM) for a in arrays]


def whole(shape):
    zeros = (0,) * len(shape)
    return pl.BlockSpec(shape, lambda *_: zeros)


def rows_of(rows, width):
    return pl.BlockSpec((rows, width), lambda s, *_: (s, 0))


def seq_of(*shape):
    tail = (0,) * len(shape)
    return pl.BlockSpec((1, *shape), lambda s, *_: (s, *tail))


MARK = sds((8, 128), F32)
MARK_SPEC = whole((8, 128))


def marked(refs):
    refs[-1][...] = jnp.zeros_like(refs[-1])
    return refs[:-1]


def head_masks():
    lanes = lax.broadcasted_iota(jnp.int32, (1, 2 * HDIM), 1)
    return lanes < HDIM, lanes >= HDIM


def pair_columns(width):
    return [slice(at, at + 2 * HDIM) for at in range(0, width, 2 * HDIM)]


def attend(q, k, v, bias, probs_ref):
    masks = head_masks()
    pieces = []
    for pair, cols in enumerate(pair_columns(q.shape[1])):
        qp, kp, vp = q[:, cols], k[:, cols], v[:, cols]
        mixed = None
        for half, mask in enumerate(masks):
            scores = mm(kp, jnp.where(mask, qp, 0), NT) + bias
            peak = jnp.max(scores, axis=0, keepdims=True)
            raised = jnp.exp(scores - peak)
            total = jnp.sum(raised, axis=0, keepdims=True)
            probs = (raised * (1.0 / total)).astype(BF)
            probs_ref[0, 2 * pair + half] = probs
            part = mm(probs, jnp.where(mask, vp, 0), TN)
            mixed = part if mixed is None else mixed + part
        pieces.append(mixed.astype(BF))
    return jnp.concatenate(pieces, axis=1)


def project(xn, sel, wq, wk, wv):
    rows = jnp.concatenate([xn, sel], axis=0)
    q = (mm(xn, wq) * SCALE).astype(BF)
    k = mm(rows, wk).astype(BF)
    v = mm(rows, wv).astype(BF)
    return q, k, v


def key_bias(seq, counts_ref, pads_ref, length):
    tokens = jnp.sum(pads_ref[pl.ds(seq, 1), :], axis=1, keepdims=True)
    token_ids = lax.broadcasted_iota(jnp.int32, (length, 1), 0)
    slot_ids = lax.broadcasted_iota(jnp.int32, (SLOT_ROWS, 1), 0)
    live = jnp.concatenate([token_ids < tokens, slot_ids < counts_ref[seq]], axis=0)
    return jnp.where(live, 0.0, -1e9).astype(F32)


def attn_first_kernel(
    first_ref, counts_ref, idx_ref, x_ref, gain_ref, pool_ref, pads_ref, wq_ref, wk_ref, wv_ref,
    xn_ref, sel_ref, bias_ref, hot_ref, q_ref, k_ref, v_ref, probs_ref, mixed_ref,
):
    seq = first_ref[0] + pl.program_id(0)
    x = x_ref[...].astype(F32)
    factor = lax.rsqrt(jnp.mean(x * x, axis=-1, keepdims=True) + EPS)
    xn = (x * factor * gain_ref[...].reshape(1, -1)).astype(BF)
    xn_ref[...] = xn
    spots = (pool_ref.shape[1], SLOT_ROWS)
    pool_ids = lax.broadcasted_iota(jnp.int32, spots, 0)
    slot_ids = lax.broadcasted_iota(jnp.int32, spots, 1)
    chosen = jnp.full(spots, -1, jnp.int32)
    for slot in range(idx_ref.shape[1]):
        chosen = jnp.where(slot_ids == slot, idx_ref[seq, slot], chosen)
    hot = jnp.where(chosen == pool_ids, 1.0, 0.0).astype(BF)
    hot_ref[0] = hot
    sel = mm(hot, pool_ref[0], TN).astype(BF)
    sel_ref[0] = sel
    bias = key_bias(seq, counts_ref, pads_ref, x_ref.shape[0])
    bias_ref[0] = bias
    q, k, v = project(xn, sel, wq_ref[...], wk_ref[...], wv_ref[...])
    q_ref[...] = q
    k_ref[0] = k
    v_ref[0] = v
    mixed_ref[...] = attend(q, k, v, bias, probs_ref)


def attn_second_kernel(
    x_ref, gain_ref, xn_ref, sel_ref, bias_ref, first_ref, wq_ref, wk_ref, wv_ref, woo_ref, wot_ref,
    q_ref, k_ref, v_ref, probs_ref, mixed_ref, middle_ref, nf_ref,
):
    q, k, v = project(xn_ref[...], sel_ref[0], wq_ref[...], wk_ref[...], wv_ref[...])
    q_ref[...] = q
    k_ref[0] = k
    v_ref[0] = v
    mixed = attend(q, k, v, bias_ref[0], probs_ref)
    mixed_ref[...] = mixed
    middle = x_ref[...].astype(F32) + mm(first_ref[...], woo_ref[...]) + mm(mixed, wot_ref[...])
    middle_ref[...] = middle
    factor = lax.rsqrt(jnp.mean(middle * middle, axis=-1, keepdims=True) + EPS)
    nf_ref[...] = (middle * factor * gain_ref[...].reshape(1, -1)).astype(BF)


def attention_forward(tokens, gain_attn, gain_ffn, pool, idx, counts, pads, seqs, mine, own, other):
    rows, width = tokens.shape
    length = rows // seqs
    keys = length + SLOT_ROWS
    inner = own[0].shape[1]
    heads = inner // HDIM
    row, head, key = rows_of(length, width), rows_of(length, inner), seq_of(keys, inner)
    kept = [
        (stored((rows, inner), BF), head),
        (stored((seqs, keys, inner), BF), key),
        (stored((seqs, keys, inner), BF), key),
        (stored((seqs, heads, keys, length), BF), seq_of(heads, keys, length)),
        (stored((rows, inner), BF), head),
    ]
    weight = whole((width, inner))
    outs = [
        (stored((rows, width), BF), row),
        (stored((seqs, SLOT_ROWS, width), BF), seq_of(SLOT_ROWS, width)),
        (stored((seqs, keys, 1), F32), seq_of(keys, 1)),
        (stored((seqs, pool.shape[1], SLOT_ROWS), BF), seq_of(pool.shape[1], SLOT_ROWS)),
        *kept,
    ]
    xn, sel, bias, hot, *first = pl.pallas_call(
        attn_first_kernel,
        grid_spec=pltpu.PrefetchScalarGridSpec(
            num_scalar_prefetch=3,
            grid=(seqs,),
            in_specs=[
                row,
                whole((width,)),
                pl.BlockSpec((1, *pool.shape[1:]), lambda s, first, *_: (first[0] + s, 0, 0)),
                whole(pads.shape),
                weight, weight, weight,
            ],
            out_specs=[o[1] for o in outs],
        ),
        out_shape=[o[0] for o in outs],
        compiler_params=params(14),
        cost_estimate=cost(12),
        name="attn_first",
    )(mine, counts, idx, *streamed(tokens, gain_attn, pool, pads, *own[:3]))
    outs = [
        *kept,
        (stored((rows, width), F32), row),
        (stored((rows, width), BF), row),
    ]
    *second, middle, nf = pl.pallas_call(
        attn_second_kernel,
        grid=(seqs,),
        out_shape=[o[0] for o in outs],
        in_specs=[
            row,
            whole((width,)),
            row,
            seq_of(SLOT_ROWS, width),
            seq_of(keys, 1),
            head,
            weight, weight, weight,
            whole((inner, width)),
            whole((inner, width)),
        ],
        out_specs=[o[1] for o in outs],
        compiler_params=params(18),
        cost_estimate=cost(12),
        name="attn_second",
    )(
        *streamed(tokens, gain_ffn),
        *streamed(xn, sel, bias, first[4]),
        *other[:3], *streamed(own[3]), other[3],
    )
    return xn, sel, hot, first, second, middle, nf


def gate_and_slope(h):
    c = 0.7978845608028654
    square = h * h
    t = jnp.tanh(h * (c + (c * 0.044715) * square))
    half = 0.5 + 0.5 * t
    slope = half + (0.5 * h) * (1.0 - t * t) * (c + (3.0 * c * 0.044715) * square)
    return h * half, slope


def ffn_kernel(own, chunk, nf_ref, cot_ref, wu_ref, wd_ref, *refs):
    rows = nf_ref.shape[0]
    units = wu_ref.shape[1]
    if own:
        got_ref, sides_ref = refs[:2]
        act_ref, di_ref, keep_ref, send_ref = marked(refs)[-4:]
    else:
        act_ref, di_ref, grad_ref = marked(refs)[-3:]
    wu, wd = wu_ref[...], wd_ref[...]
    for r in range(rows // chunk):
        at = slice(r * chunk, (r + 1) * chunk)
        act, slope = gate_and_slope(mm(nf_ref[at], wu))
        act_ref[at] = act.astype(BF)
        di_ref[at] = (mm(cot_ref[at], wd, NT) * slope).astype(BF)
    at = pl.ds(pl.multiple_of(pl.program_id(0) * units, units), units)
    down = mm(act_ref[...], cot_ref[...], TN).astype(BF)
    up = mm(nf_ref[...], di_ref[...], TN).astype(BF)
    if not own:
        grad_ref[0, at] = down
        grad_ref[1, :, at] = up
        return
    down = bf_sum(down, got_ref[0, at])
    up = bf_sum(up, got_ref[1, :, at])
    upper = sides_ref[0] == 1

    @pl.when(upper)
    def _():
        keep_ref[:, at] = up
        send_ref[at] = down

    @pl.when(jnp.logical_not(upper))
    def _():
        keep_ref[at] = down
        send_ref[:, at] = up


def ffn_part(index, nf, cot, weights, sums=(), after=()):
    rows, width = nf.shape
    own = len(sums) > 0
    units = 256
    steps = width // units
    full, square, part = whole((rows, width)), (width, width), pl.BlockSpec((rows, units), lambda j: (0, j))
    grads = [sds(square, BF)] * 2 if own else [sds((2, *square), BF)]
    extra = [whole((2, *square)), IN_SMEM] if own else []
    return pl.pallas_call(
        functools.partial(ffn_kernel, own, 256),
        grid=(steps,),
        out_shape=[*[stored((rows, width), BF)] * 2, *grads, MARK],
        in_specs=[
            full,
            full,
            pl.BlockSpec((width, units), lambda j: (0, index * steps + j)),
            pl.BlockSpec((units, width), lambda j: (index * steps + j, 0)),
            *extra,
            *[ANYWHERE] * len(after),
        ],
        out_specs=[part, part, *[whole(g.shape) for g in grads], MARK_SPEC],
        compiler_params=params(26),
        cost_estimate=cost(10),
        name="ffn_part",
    )(*streamed(nf, cot), *weights, *sums, *after)


def norm_back_kernel(cot_ref, middle_ref, gain_ref, wut_ref, wuo_ref, d0t, d0o, d1t, d1o, *refs):
    gm_ref, gmb_ref, gg_ref = marked(refs)[-3:]
    middle = middle_ref[...]
    width = middle.shape[1]
    dnf = 0.0
    for at, parts in enumerate(((d0t, d0o), (d1t, d1o))):
        cols = slice(at * width, (at + 1) * width)
        for part, wu_ref in zip(parts, (wut_ref, wuo_ref)):
            dnf += mm(part[...], wu_ref[:, cols], NT)
    factor = lax.rsqrt(jnp.mean(middle * middle, axis=-1, keepdims=True) + EPS)
    scaled = middle * factor
    e = gain_ref[...].reshape(1, -1) * dnf
    inner_mean = jnp.mean(e * scaled, axis=-1, keepdims=True)
    gm = cot_ref[...].astype(F32) + factor * (e - scaled * inner_mean)
    gm_ref[...] = gm
    gmb_ref[...] = gm.astype(BF)
    total = jnp.sum(dnf * scaled, axis=0, keepdims=True)
    gg_ref[...] = jnp.where(pl.program_id(0) == 0, 0.0, gg_ref[...]) + total


def norm_back(cot, middle, gain_ffn, wu_oth, wu_own, dis, after=()):
    rows, width = cot.shape
    block = 256
    row = rows_of(block, width)
    return pl.pallas_call(
        norm_back_kernel,
        grid=(rows // block,),
        out_shape=[stored((rows, width), F32), stored((rows, width), BF), sds((1, width), F32), MARK],
        in_specs=[
            row, row, whole((width,)), whole(wu_own.shape), whole(wu_own.shape), row, row, row, row,
            *[ANYWHERE] * len(after),
        ],
        out_specs=[row, row, whole((1, width)), MARK_SPEC],
        compiler_params=params(22),
        cost_estimate=cost(0.1),
        name="norm_back",
    )(*streamed(cot, middle, gain_ffn), wu_oth, *streamed(wu_own, *dis), *after)


def block_out_kernel(middle_ref, wdt_ref, wdo_ref, a0t, a0o, a1t, a1o, *refs):
    total = middle_ref[...]
    width = total.shape[1]
    for at, parts in enumerate(((a0t, a0o), (a1t, a1o))):
        for part, wd_ref in zip(parts, (wdt_ref, wdo_ref)):
            total += mm(part[...], wd_ref[at * width : (at + 1) * width])
    marked(refs)[-1][...] = total.astype(BF)


def block_output(middle, wd_oth, wd_own, acts, after=()):
    rows, width = middle.shape
    block = 256
    row = rows_of(block, width)
    return pl.pallas_call(
        block_out_kernel,
        grid=(rows // block,),
        out_shape=[stored((rows, width), BF), MARK],
        in_specs=[
            row, whole(wd_own.shape), whole(wd_own.shape), row, row, row, row, *[ANYWHERE] * len(after),
        ],
        out_specs=[row, MARK_SPEC],
        compiler_params=params(18),
        cost_estimate=cost(0.1),
        name="block_out",
    )(*streamed(middle), wd_oth, *streamed(wd_own, *acts), *after)


def stack(grad):
    part = grad.shape[1]
    return jnp.concatenate([grad[at : at + part] for at in range(0, grad.shape[0], part)], axis=1)


def unstack_to(ref, at, stacked):
    part = stacked.shape[0]
    for block in range(stacked.shape[1] // part):
        rows = slice(block * part, (block + 1) * part)
        ref[rows, at : at + part] = stacked[:, rows].astype(F32)


def attn_back_kernel(
    gm_ref, xn_ref, selall_ref, wo_ref, q_ref, k_ref, v_ref, p_ref, m_ref, *refs
):
    awo, aw, slots = refs[-3:]
    dq_ref, dk_ref, dv_ref, grad_ref = marked(refs[:-3])[-4:]
    step = pl.program_id(0)
    masks = head_masks()
    gm, xn = gm_ref[...], xn_ref[...]
    length = gm.shape[0]

    @pl.when(step == 0)
    def _():
        awo[...] = jnp.zeros_like(awo)
        aw[...] = jnp.zeros_like(aw)

    awo[...] += mm(m_ref[...], gm, TN)
    dmix = mm(gm, wo_ref[...], NT).astype(BF)
    dqs, dks, dvs = [], [], []
    for pair, cols in enumerate(pair_columns(dmix.shape[1])):
        qp, kp, vp, dp = q_ref[:, cols], k_ref[0, :, cols], v_ref[0, :, cols], dmix[:, cols]
        dq = dk = dv = 0.0
        for half, mask in enumerate(masks):
            probs = p_ref[0, 2 * pair + half]
            dp_head = jnp.where(mask, dp, 0)
            weighted = mm(vp, dp_head, NT)
            high = probs.astype(F32)
            delta = jnp.sum(high * weighted, axis=0, keepdims=True)
            ds = (high * (weighted - delta)).astype(BF)
            dv += mm(probs, dp_head)
            dq += mm(ds, jnp.where(mask, kp, 0), TN)
            dk += mm(ds, jnp.where(mask, qp, 0))
        dqs.append((dq * SCALE).astype(BF))
        dks.append(dk.astype(BF))
        dvs.append(dv.astype(BF))
    dq, dk, dv = [jnp.concatenate(d, axis=1) for d in (dqs, dks, dvs)]
    dq_ref[...] = dq
    dk_ref[0] = dk
    dv_ref[0] = dv
    aw[...] += mm(xn, jnp.concatenate([dq, dk[:length], dv[:length]], axis=1), TN)
    at = pl.ds(pl.multiple_of(step * SLOT_ROWS, SLOT_ROWS), SLOT_ROWS)
    slots[at] = jnp.concatenate([dk[length:], dv[length:]], axis=1)

    @pl.when(step == pl.num_programs(0) - 1)
    def _():
        inner = awo.shape[0]
        grad_ref[:inner] = awo[...].astype(BF)
        grad_ref[inner : 2 * inner] = stack(aw[:, :inner].astype(BF))
        rest = (aw[:, inner:] + mm(selall_ref[...], slots[...], TN)).astype(BF)
        grad_ref[2 * inner : 3 * inner] = stack(rest[:, :inner])
        grad_ref[3 * inner :] = stack(rest[:, inner:])


def attn_back(gmb, xn, sel, wo, kept, at, inner, us, after=()):
    rows, width = gmb.shape
    seqs, _, keys, length = kept[3].shape
    heads = inner // HDIM
    block = at // inner
    row = rows_of(length, width)
    head_in = pl.BlockSpec((length, inner), lambda s: (s, block))
    key_in = pl.BlockSpec((1, keys, inner), lambda s: (s, 0, block))
    grads = sds((4 * inner, width), BF)
    outs = [
        (stored((rows, inner), BF), rows_of(length, inner)),
        (stored((seqs, keys, inner), BF), seq_of(keys, inner)),
        (stored((seqs, keys, inner), BF), seq_of(keys, inner)),
        (grads, whole(grads.shape)),
        (MARK, MARK_SPEC),
    ]
    return pl.pallas_call(
        attn_back_kernel,
        grid=(seqs,),
        out_shape=[o[0] for o in outs],
        in_specs=[
            row, row, whole((seqs * SLOT_ROWS, width)),
            pl.BlockSpec((inner, width), lambda s: (block, 0)),
            head_in, key_in, key_in,
            pl.BlockSpec((1, heads, keys, length), lambda s: (s, block, 0, 0)),
            head_in, *[ANYWHERE] * len(after),
        ],
        out_specs=[o[1] for o in outs],
        scratch_shapes=[
            pltpu.VMEM((inner, width), F32),
            pltpu.VMEM((width, 3 * inner), F32),
            pltpu.VMEM((seqs * SLOT_ROWS, 2 * inner), BF),
        ],
        compiler_params=params(22),
        cost_estimate=cost(us),
        name="attn_back",
    )(*streamed(gmb, xn, sel.reshape(seqs * SLOT_ROWS, width)), wo, *streamed(*kept), *after)


def input_back_kernel(
    parts, x_ref, gm_ref, gain_ref, hot_ref, wqo, wqt, wko, wkt, wvo, wvt,
    *refs,
):
    grads, refs = refs[: 3 * parts], refs[3 * parts :]
    dq = jnp.concatenate([g[...] for g in grads[:parts]], axis=1)
    dk = jnp.concatenate([g[0] for g in grads[parts : 2 * parts]], axis=1)
    dv = jnp.concatenate([g[0] for g in grads[2 * parts :]], axis=1)
    wq, wk, wv = refs[-3:]
    gx_ref, gp_ref, gg_ref = marked(refs[:-3])[-3:]
    first = pl.program_id(0) == 0
    inner = wqo.shape[1]
    length = x_ref.shape[0]

    @pl.when(first)
    def _():
        for cat, own, oth in ((wq, wqo, wqt), (wk, wko, wkt), (wv, wvo, wvt)):
            cat[:, :inner] = own[...]
            cat[:, inner:] = oth[...]

    dkeys = mm(dk, wk[...], NT) + mm(dv, wv[...], NT)
    dxn = dkeys[:length] + mm(dq, wq[...], NT)
    x = x_ref[...].astype(F32)
    factor = lax.rsqrt(jnp.mean(x * x, axis=-1, keepdims=True) + EPS)
    scaled = x * factor
    c = gain_ref[...].reshape(1, -1) * dxn
    inner_mean = jnp.mean(c * scaled, axis=-1, keepdims=True)
    gx_ref[...] = gm_ref[...] + factor * (c - scaled * inner_mean)
    total = jnp.sum(dxn * scaled, axis=0, keepdims=True)
    gg_ref[...] = jnp.where(first, 0.0, gg_ref[...]) + total
    gp_ref[0] = mm(hot_ref[0], dkeys[length:].astype(BF))


def input_back(tokens, gm, gain_attn, hot, own, oth, grads, after=()):
    rows, width = tokens.shape
    seqs, keys = grads[0][1].shape[:2]
    length = rows // seqs
    pool_rows, inner = hot.shape[1], own[0].shape[1]
    row = rows_of(length, width)
    flat = [g[kind] for kind in range(3) for g in grads]
    return pl.pallas_call(
        functools.partial(input_back_kernel, len(grads)),
        grid=(seqs,),
        out_shape=[
            stored((rows, width), F32),
            sds((seqs, pool_rows, width), F32),
            sds((1, width), F32),
            MARK,
        ],
        in_specs=[
            row, row, whole((width,)), seq_of(pool_rows, SLOT_ROWS),
            *[whole((width, inner))] * 6,
            *[rows_of(length, g[0].shape[1]) for g in grads],
            *[seq_of(keys, g[0].shape[1]) for g in [*grads, *grads]],
            *[ANYWHERE] * len(after),
        ],
        out_specs=[row, seq_of(pool_rows, width), whole((1, width)), MARK_SPEC],
        scratch_shapes=[pltpu.VMEM((width, 2 * inner), BF)] * 3,
        compiler_params=params(22),
        cost_estimate=cost(0.1),
        name="input_back",
    )(
        *streamed(tokens, gm, gain_attn, hot),
        *[w for pair in zip(streamed(*own[:3]), oth[:3]) for w in pair],
        *streamed(*flat), *after,
    )


def bf_sum(a, b):
    return (a.astype(F32) + b.astype(F32)).astype(BF)


def grid_steps(rows):
    return next((n for n in (4, 2) if rows % (16 * n) == 0 and rows // n >= 96), 1)


def halve_kernel(level, sides_ref, a_ref, b_ref, *refs):
    keep_ref, send_ref = marked(refs)[-2:]
    low, high = bf_sum(a_ref[0], b_ref[0]), bf_sum(a_ref[1], b_ref[1])
    upper = sides_ref[level] == 1
    keep_ref[...] = jnp.where(upper, high, low)
    send_ref[...] = jnp.where(upper, low, high)


def halve(level, sides, a, b, after=()):
    rows, width = a.shape[0] // 2, a.shape[1]
    steps = grid_steps(rows)
    pair = pl.BlockSpec((2, rows // steps, width), lambda j: (0, j, 0))
    half = rows_of(rows // steps, width)
    return pl.pallas_call(
        functools.partial(halve_kernel, level),
        grid=(steps,),
        out_shape=[sds((rows, width), BF)] * 2 + [MARK],
        in_specs=[IN_SMEM, pair, pair, *[ANYWHERE] * len(after)],
        out_specs=[half, half, MARK_SPEC],
        compiler_params=params(6),
        cost_estimate=cost(0.05),
        name="halve",
    )(sides, a.reshape(2, rows, width), b.reshape(2, rows, width), *after)


def open_kernel(sides_ref, *refs):
    keep_ref, send_ref = marked(refs)[-2:]
    upper = sides_ref[0] == 1
    at = 0
    for own_ref, got_ref in zip(refs[::2], refs[1::2]):
        if len(own_ref.shape) != 3 or at == keep_ref.shape[0]:
            break
        rows = own_ref.shape[1]
        low, high = bf_sum(own_ref[0], got_ref[0]), bf_sum(own_ref[1], got_ref[1])
        keep_ref[at : at + rows] = jnp.where(upper, high, low)
        send_ref[at : at + rows] = jnp.where(upper, low, high)
        at += rows


def open_sums(sides, owns, gots, after=()):
    width = owns[0].shape[1]
    arrays = [a.reshape(2, -1, width) for pair in zip(owns, gots) for a in pair]
    rows = sum(o.shape[0] for o in owns) // 2
    return pl.pallas_call(
        open_kernel,
        out_shape=[sds((rows, width), BF)] * 2 + [MARK],
        in_specs=[IN_SMEM, *[whole(a.shape) for a in arrays], *[ANYWHERE] * len(after)],
        out_specs=[whole((rows, width))] * 2 + [MARK_SPEC],
        compiler_params=params(14),
        cost_estimate=cost(0.05),
        name="open_sums",
    )(sides, *arrays, *after)


def add_kernel(a_ref, b_ref, *refs):
    marked(refs)[-1][...] = (a_ref[...].astype(F32) + b_ref[...].astype(F32)).astype(a_ref.dtype)


def add(a, b, after=()):
    full = whole(a.shape)
    return pl.pallas_call(
        add_kernel,
        out_shape=[sds(a.shape, a.dtype), MARK],
        in_specs=[full, full, *[ANYWHERE] * len(after)],
        out_specs=[full, MARK_SPEC],
        compiler_params=params(2),
        cost_estimate=cost(0.05),
        name="add",
    )(a, b, *after)


def joined(level, sides_ref, mine, got):
    upper = sides_ref[level] == 1
    return jnp.where(upper, got, mine), jnp.where(upper, mine, got)


def join_kernel(level, sides_ref, mine_ref, got_ref, *refs):
    out_ref = marked(refs)[-1]
    out_ref[0], out_ref[1] = joined(level, sides_ref, mine_ref[...], got_ref[...])


def join(level, sides, mine, got, after=()):
    rows, width = mine.shape
    steps = grid_steps(rows)
    part = rows_of(rows // steps, width)
    both, mark = pl.pallas_call(
        functools.partial(join_kernel, level),
        grid=(steps,),
        out_shape=[sds((2, rows, width), BF), MARK],
        in_specs=[IN_SMEM, part, part, *[ANYWHERE] * len(after)],
        out_specs=[pl.BlockSpec((2, rows // steps, width), lambda j: (0, j, 0)), MARK_SPEC],
        compiler_params=params(6),
        cost_estimate=cost(0.05),
        name="join",
    )(sides, mine, got, *after)
    return both.reshape(2 * rows, width), mark


def pool_join_kernel(mine_ref, got_ref, *refs):
    out_ref = marked(refs)[-1]
    first = lax.axis_index("mp") == 0
    mine, got = mine_ref[...], got_ref[...]
    seqs = mine.shape[0]
    out_ref[:seqs] = jnp.where(first, mine, got)
    out_ref[seqs:] = jnp.where(first, got, mine)


def pool_join(mine, got, after=()):
    full, shape = whole(mine.shape), (2 * mine.shape[0], *mine.shape[1:])
    return pl.pallas_call(
        pool_join_kernel,
        out_shape=[stored(shape, F32), MARK],
        in_specs=[full, full, *[ANYWHERE] * len(after)],
        out_specs=[whole(shape), MARK_SPEC],
        compiler_params=params(6),
        cost_estimate=cost(1),
        name="pool_join",
    )(mine, got, *after)


def ffn_finish_kernel(sides_ref, mine_ref, got_ref, *refs):
    down_ref, up_ref = marked(refs)[-2:]
    down, up = joined(0, sides_ref, mine_ref[...], got_ref[...])
    down_ref[...] = down.astype(F32)
    up_ref[...] = up.astype(F32)


def ffn_finish(index, count, sides, mine, got, before=(), after=()):
    width = mine.shape[1]
    steps = 4
    part = rows_of(width // steps, width)
    shapes = [stored((count * width, width), F32), stored((width, count * width), F32)]
    return pl.pallas_call(
        ffn_finish_kernel,
        grid=(steps,),
        out_shape=[*shapes, MARK],
        in_specs=[IN_SMEM, part, part, *[ANYWHERE] * (len(before) + len(after))],
        out_specs=[
            pl.BlockSpec((width // steps, width), lambda j: (index * steps + j, 0)),
            pl.BlockSpec((width // steps, width), lambda j: (j, index)),
            MARK_SPEC,
        ],
        input_output_aliases={3 + at: at for at in range(len(before))},
        compiler_params=params(10),
        cost_estimate=cost(0.05),
        name="ffn_finish",
    )(sides, mine, got, *before, *after)


def attn_finish_kernel(parts, sides_ref, mine_ref, got_ref, *refs):
    wq_ref, wk_ref, wv_ref, wo_ref = refs[-4:]
    low, high = joined(0, sides_ref, mine_ref[...], got_ref[...])
    at = column = 0
    for part in parts:
        wo_ref[column : column + part] = low[at : at + part].astype(F32)
        unstack_to(wq_ref, column, low[at + part : at + 2 * part])
        unstack_to(wk_ref, column, high[at : at + part])
        unstack_to(wv_ref, column, high[at + part : at + 2 * part])
        at, column = at + 2 * part, column + part


def attn_finish(parts, sides, mine, got, after=()):
    rows, width = mine.shape
    inner = rows // 2
    full = whole(mine.shape)
    return pl.pallas_call(
        functools.partial(attn_finish_kernel, parts),
        out_shape=[stored((width, inner), F32)] * 3 + [stored((inner, width), F32)],
        in_specs=[IN_SMEM, full, full, *[ANYWHERE] * len(after)],
        out_specs=[whole((width, inner))] * 3 + [whole((inner, width))],
        compiler_params=params(14),
        cost_estimate=cost(2),
        name="attn_finish",
    )(sides, mine, got, *after)


class ChipSum:
    def __init__(self, dp, mp):
        bits = dp.bit_length() - 1
        here = lax.axis_index("dp")
        bit = [(here >> b) & 1 for b in range(bits)]
        if bits == 4:
            orders = ([1, 2, 4, 12], [2, 1, 12, 4])
            sides = (
                [bit[0], bit[1], bit[2] ^ bit[3], bit[3]],
                [bit[1], bit[0], bit[3], bit[2]],
            )
        else:
            swap = list(range(bits))
            swap[:2] = swap[:2][::-1]
            orders = ([1 << b for b in range(bits)], [1 << b for b in swap])
            sides = (bit, [bit[b] for b in swap])
        second = lax.axis_index("mp") % 2 == 1
        self.sides = jnp.where(second, jnp.stack(sides[1]), jnp.stack(sides[0]))
        self.levels = bits
        self.pairs = [
            [
                (d * mp + m, (d ^ orders[m % 2][b]) * mp + m)
                for d in range(dp)
                for m in range(mp)
            ]
            for b in range(bits)
        ]

        masks = [1 << b for b in range(bits)]
        self.turns = [
            [(d * mp + m, (d ^ mask) * mp + m) for d in range(dp) for m in range(mp)]
            for mask in masks[:1] + masks[2:] + masks[1:2]
        ]

    def turn(self, at, array):
        return lax.ppermute(array, ("dp", "mp"), self.turns[at])

    def exchange(self, level, array):
        return lax.ppermute(array, ("dp", "mp"), self.pairs[level])


class Group:
    def __init__(self, chips, mine, got, at=0):
        self.chips, self.mine, self.got, self.at = chips, mine, got, at

    @property
    def done(self):
        return self.at == 2 * self.chips.levels

    def step(self, after=()):
        chips, levels = self.chips, self.chips.levels
        level = self.at if self.at < levels else 2 * levels - 1 - self.at
        if self.at < levels:
            self.mine, sent, mark = halve(level, chips.sides, self.mine, self.got, after)
        elif self.at == levels:
            self.mine, mark = add(self.mine, self.got, after)
            sent = self.mine
        else:
            self.mine, mark = join(level + 1, chips.sides, self.mine, self.got, after)
            sent = self.mine
        self.got = chips.exchange(level, sent)
        self.at += 1
        return [mark]


class Small:
    def __init__(self, chips, array, got):
        self.chips, self.mine, self.got, self.at = chips, array, got, -1

    @property
    def done(self):
        return self.at == self.chips.levels

    def step(self, after=()):
        self.mine, mark = add(self.mine, self.got, after)
        self.at += 1
        if not self.done:
            self.got = self.chips.turn(self.at, self.mine)
        return [mark]


def arrived(groups):
    return [g.got for g in groups]


def body(
    dp, mp, tokens, cotangent, w_query, key_projection_weight, value_projection_weight, w_out,
    w_up, w_down, gain_attn, gain_ffn, value_pool, slot_index, slot_count, pad_mask,
):
    seqs = tokens.shape[0] // pad_mask.shape[1]
    mine = (lax.axis_index("mp") * seqs)[None]

    def core_swap(array):
        return lax.ppermute(array, "mp", [(i, i ^ 1) for i in range(mp)])

    own = (w_query, key_projection_weight, value_projection_weight, w_out)
    oth = tuple(core_swap(w) for w in own)
    wu_oth, wd_oth = core_swap(w_up), core_swap(w_down)
    xn, sel, hot, first, second, middle, nf = attention_forward(
        tokens, gain_attn, gain_ffn, value_pool, slot_index, slot_count, pad_mask, seqs, mine,
        own, oth,
    )
    chips = ChipSum(dp, mp)
    count = w_up.shape[1] // w_up.shape[0]
    weights_oth, weights_own = (wu_oth, wd_oth), streamed(w_up, w_down)
    acts, dis, swapped, ffn, mark = [], [], [], [], []
    for at in range(count):
        act, di, grad, mark = ffn_part(at, nf, cotangent, weights_oth, (), mark)
        acts.append([act])
        dis.append([di])
        swapped.append(core_swap(grad))
        mark = [mark]
    for at in range(count):
        act, di, keep, send, mark = ffn_part(
            at, nf, cotangent, weights_own, (swapped[at], chips.sides), mark
        )
        acts[at].append(act)
        dis[at].append(di)
        ffn.append(Group(chips, keep, chips.exchange(0, send), 1))
        mark = [mark]
    acts, dis = sum(acts, []), sum(dis, [])
    gm, gmb, gg_ffn, mark = norm_back(cotangent, middle, gain_ffn, wu_oth, w_up, dis, mark)
    mark = ffn[0].step([mark])
    parts, starts = (256, 128), (0, 256)
    assert sum(parts) == w_out.shape[0]
    d_own, d_oth, a_own, a_got = [], [], [], []
    for at, part in zip(starts, parts):
        *d, grad, mark = attn_back(gmb, xn, sel, oth[3], second, at, part, 0.1, mark)
        d_oth.append(d)
        a_got.append(core_swap(grad))
        mark = ffn[1].step(ffn[0].step([mark, *arrived(ffn)]))
    for at, part in zip(starts, parts):
        *d, grad, mark = attn_back(
            gmb, xn, sel, *streamed(w_out), first, at, part, 22, mark
        )
        d_own.append(d)
        a_own.append(grad)
        if len(a_own) < len(parts):
            mark = ffn[1].step(ffn[0].step([mark, *arrived(ffn)]))
    keep, send, mark = open_sums(chips.sides, a_own, a_got, [mark, *arrived(ffn)])
    attn = Group(chips, keep, chips.exchange(0, send), 1)
    mark = ffn[1].step(ffn[0].step([mark]))
    grad_tokens, grad_pool, gg_attn, mark = input_back(
        tokens, gm, gain_attn, hot, own, oth, [*d_own, *d_oth], mark
    )
    pool_got = core_swap(grad_pool)
    gains = jnp.concatenate([gg_attn, gg_ffn], axis=0)
    gains = Small(chips, gains, core_swap(gains))
    mark = gains.step(ffn[1].step(ffn[0].step(attn.step([mark, *arrived(ffn)]))))
    block_out = None
    last = 2 * chips.levels
    ready = []
    late = [0] * count
    while attn.at < last or not gains.done:
        waited = [g for g, l in zip(ffn, late) if g.at < last or l == 1]
        late = [l + (g.at == last) for g, l in zip(ffn, late)]
        if attn.at < last:
            mark = attn.step([*mark, *arrived([*waited, *([] if gains.done else [gains])])])
        for group in ffn:
            if group.at < last:
                mark = group.step(mark)
        if not gains.done:
            mark = gains.step(mark)
        if block_out is None:
            block_out, mark = block_output(middle, wd_oth, w_down, acts, mark)
            grad_value_pool, mark = pool_join(grad_pool, pool_got, [mark])
            mark = [mark]
    while len(ready) < count:
        at = len(ready)
        *out, mark = ffn_finish(
            at, count, chips.sides, ffn[at].mine, ffn[at].got, ready[-1] if ready else (), mark
        )
        ready.append(out)
        mark = [mark]
    grad_wd, grad_wu = ready[-1]
    grad_wq, grad_wk, grad_wv, grad_wo = attn_finish(parts, chips.sides, attn.mine, attn.got, mark)
    return (
        block_out, grad_tokens, grad_wq, grad_wk, grad_wv, grad_wo, grad_wu, grad_wd,
        gains.mine[0], gains.mine[1], grad_value_pool,
    )


def solution(mesh):
    placed = (
        P(("dp", "mp"), None),
        P(("dp", "mp"), None),
        P(None, "mp"),
        P(None, "mp"),
        P(None, "mp"),
        P("mp", None),
        P(None, "mp"),
        P("mp", None),
        P(),
        P(),
        P("dp", None, None),
        P("dp", None),
        P("dp"),
        P("dp", None),
    )
    return jax.shard_map(
        functools.partial(body, mesh.shape["dp"], mesh.shape["mp"]),
        mesh=mesh,
        in_specs=placed,
        out_specs=(
            P(("dp", "mp"), None),
            P(("dp", "mp"), None),
            P(None, "mp"),
            P(None, "mp"),
            P(None, "mp"),
            P("mp", None),
            P(None, "mp"),
            P("mp", None),
            P(),
            P(),
            P("dp", None, None),
        ),
        check_vma=False,
    )
```
